32 devices in a mesh: lon: 4 (over x, core), lat: 8 (over z, y).
Axes of the slice: x: 2, y: 2, z: 4, core: 2. Of those that a mesh axis runs over, the one named last changes fastest.
Arguments:
- tracers: float32 [2, 20, 512, 1536], P(None, None, 'lat', 'lon'), may hold values from -6 to 6
- east_velocity: bfloat16 [20, 512, 1536], P(None, 'lat', 'lon'), may hold values from -3 to 3
- north_velocity: bfloat16 [20, 512, 1536], P(None, 'lat', 'lon'), may hold values from -3 to 3
- vertical_diffusivity: bfloat16 [20, 512, 1536], P(None, 'lat', 'lon'), may hold values from 0.049804688 to 5
- depth_levels: int32 [512, 1536], P('lat', 'lon'), may hold values from 0 to 20
- ocean_blocks: int32 [16, 8], P('lat', 'lon'), may hold values 0 or 1
- forcing: float32 [512, 1536], P('lat', 'lon'), may hold values from -6 to 6
- surface_coupling: float32 [512, 1536], P('lat', 'lon'), may hold values from 0.1 to 2
Outputs:
- new_tracers: float32 [2, 20, 512, 1536], P(None, None, 'lat', 'lon')
- surface_solution: float32 [512, 1536], P('lat', 'lon')
The draws below stay inside these ranges and needn't reach their ends.
All inputs are finite; a program needn't handle non-finite values. No bound on the sum of `ocean_blocks` on one device may be relied on, other than what follows from the above.
Results may differ from the reference program's by a relative error of at most 0.0003.
Values sent between devices are 32-bit elements; how exact they have to be, the bound alone decides.
A program may use at most 192 MiB of HBM per device.

```python
import math
import jax
import jax.numpy as jnp
from jax import lax

LEV = 20
NTRA = 2
ITERS = 3
NX = 1536
NY = 512
NBX = 8
NBY = 16


def plant(values, rng, low, top_value):
    longest = values.shape.index(max(values.shape))
    spots = []
    for shift in (0, 1):
        where = [jax.random.randint(jax.random.fold_in(rng, axis), (), 0, length) for axis, length in enumerate(values.shape)]
        where[longest] = (where[longest] + shift) % values.shape[longest]
        spots.append(tuple(where))
    return values.at[spots[0]].set(low).at[spots[1]].set(top_value)


def shard_levels(rng, dims, cuts, smallest, largest):
    level, own = 1.0, jax.random.fold_in(rng, 6)
    for position, parts in cuts:
        steps = jnp.exp(jax.random.uniform(jax.random.fold_in(own, position), (parts,), jnp.float32, smallest / len(cuts), largest / len(cuts)))
        level = level * jnp.repeat(steps, dims[position] // parts).reshape([-1 if axis == position else 1 for axis in range(len(dims))])
    return level


def normal_values(key, extent, deviation, bound, shards=(), held_as=jnp.bfloat16):
    values = deviation * jax.random.normal(key, extent, jnp.float32)
    if shards:
        values = values * shard_levels(key, extent, shards, -0.22, 0.18)
    return jnp.clip(values, -bound, bound).astype(held_as)


def setup_inputs(seed: int = 0) -> dict:
    splits = jax.random.split(jax.random.key(seed), 9)
    return {
        "tracers": normal_values(splits[0], (NTRA, LEV, NY, NX), 1.0, 6.0, ((2, 8), (3, 4)), jnp.float32),
        "east_velocity": normal_values(splits[1], (LEV, NY, NX), 0.5, 3.0, ((1, 8), (2, 4))),
        "north_velocity": normal_values(splits[2], (LEV, NY, NX), 0.5, 3.0, ((1, 8), (2, 4))),
        "vertical_diffusivity": jnp.clip(jnp.exp(math.log(5.0) - 4.609084 * jax.random.uniform(splits[3], (LEV, NY, NX), jnp.float32) ** shard_levels(splits[3], (LEV, NY, NX), ((1, 8), (2, 4)), -0.2, 0.2)), 0.049804688, 5.0).astype(jnp.bfloat16),
        "depth_levels": plant(jax.random.randint(splits[4], (NY, NX), 0, LEV + 1), jax.random.fold_in(splits[4], 1), 0, LEV).astype(jnp.int32),
        "ocean_blocks": plant((jax.random.randint(splits[5], (NBY, NBX), 0, 4) < 3).astype(jnp.int32), jax.random.fold_in(splits[5], 1), 0, 1),
        "forcing": normal_values(splits[6], (NY, NX), 1.0, 6.0, ((0, 8), (1, 4)), jnp.float32),
        "surface_coupling": jnp.clip(jnp.exp(math.log(2.0) - 2.9957323 * jax.random.uniform(splits[7], (NY, NX), jnp.float32) ** shard_levels(splits[7], (NY, NX), ((0, 8), (1, 4)), -0.2, 0.2)), 0.1, 2.0),
    }


advection_rate = 0.25
biharmonic_rate = 0.01
corner_weight = 0.5


def window(array, shift_row, shift_col):
    inner_height = array.shape[-2] - 2
    inner_width = array.shape[-1] - 2
    return array[..., shift_row:shift_row + inner_height, shift_col:shift_col + inner_width]


def masked_laplacian(values, wet_mask):
    centre = window(values, 1, 1)
    running = jnp.zeros_like(centre)
    for shift_row, shift_col in ((0, 1), (2, 1), (1, 0), (1, 2)):
        running = running + window(wet_mask, shift_row, shift_col) * (window(values, shift_row, shift_col) - centre)
    return window(wet_mask, 1, 1) * running


def face_flux(speed_one, speed_two, tracer_one, tracer_two, wet_one, wet_two):
    return 0.5 * (speed_one + speed_two) * 0.5 * (tracer_one + tracer_two) * wet_one * wet_two


def baroclinic(padded):
    tracer = padded[0:2]
    wet_mask = padded[2]
    inner_tracer = tracer[..., 1:-1, 1:-1]
    inner_mask = wet_mask[..., 1:-1, 1:-1]
    east_speed = padded[3][..., 1:-1, 1:-1]
    north_speed = padded[4][..., 1:-1, 1:-1]
    lap_one = masked_laplacian(tracer, wet_mask)
    lap_two = masked_laplacian(lap_one, inner_mask)
    centre = window(inner_tracer, 1, 1)
    wet_centre = window(inner_mask, 1, 1)
    east_flux = face_flux(window(east_speed, 1, 1), window(east_speed, 1, 2), centre, window(inner_tracer, 1, 2), wet_centre, window(inner_mask, 1, 2))
    west_flux = face_flux(window(east_speed, 1, 0), window(east_speed, 1, 1), window(inner_tracer, 1, 0), centre, window(inner_mask, 1, 0), wet_centre)
    north_flux = face_flux(window(north_speed, 1, 1), window(north_speed, 2, 1), centre, window(inner_tracer, 2, 1), wet_centre, window(inner_mask, 2, 1))
    south_flux = face_flux(window(north_speed, 0, 1), window(north_speed, 1, 1), window(inner_tracer, 0, 1), centre, window(inner_mask, 0, 1), wet_centre)
    divergence = east_flux - west_flux + north_flux - south_flux
    return wet_centre * (centre - advection_rate * divergence - biharmonic_rate * lap_two)


def vertical_mix(values, wet_mask, diffusivity):
    level_count = wet_mask.shape[0]
    zeros_plane = jnp.zeros_like(wet_mask[0])
    coupling = [zeros_plane] + [diffusivity[k] * wet_mask[k] * wet_mask[k - 1] for k in range(1, level_count)] + [zeros_plane]
    upper_ratio = []
    reduced = []
    for k in range(level_count):
        diagonal = 1.0 + coupling[k] + coupling[k + 1]
        if k == 0:
            divisor = diagonal
            source = values[:, 0]
        else:
            divisor = diagonal + coupling[k] * upper_ratio[k - 1]
            source = values[:, k] + coupling[k] * reduced[k - 1]
        upper_ratio.append(-coupling[k + 1] / divisor)
        reduced.append(source / divisor)
    result = [reduced[-1]]
    for k in range(level_count - 2, -1, -1):
        result.insert(0, reduced[k] - upper_ratio[k] * result[0])
    return jnp.stack(result, axis=1)


def nine_point(padded, wet_surface, centre_weight):
    centre = window(padded, 1, 1)
    edges = window(padded, 0, 1) + window(padded, 2, 1) + window(padded, 1, 0) + window(padded, 1, 2)
    corners = window(padded, 0, 0) + window(padded, 0, 2) + window(padded, 2, 0) + window(padded, 2, 2)
    return wet_surface * (centre_weight * centre - edges - corner_weight * corners)


def fold_pad(array, margin, fold_signs):
    widened = jnp.concatenate([array[..., -margin:], array, array[..., :margin]], axis=-1)
    southern = jnp.zeros(widened.shape[:-2] + (margin, widened.shape[-1]), widened.dtype)
    northern = jnp.flip(widened[..., -margin:, :], axis=(-2, -1)) * fold_signs
    return jnp.concatenate([southern, widened, northern], axis=-2)


def reference(tracers, east_velocity, north_velocity, vertical_diffusivity, depth_levels, ocean_blocks, forcing, surface_coupling):
    ocean_cells = jnp.repeat(jnp.repeat(ocean_blocks, NY // NBY, axis=0), NX // NBX, axis=1).astype(jnp.float32)
    fold_signs = jnp.array([1.0, 1.0, 1.0, -1.0, -1.0], jnp.float32).reshape(5, 1, 1)

    def level_update(k):
        tracer_level = lax.dynamic_index_in_dim(tracers, k, 1, keepdims=False)
        wet_level = jnp.where(k < depth_levels, ocean_cells, jnp.zeros_like(ocean_cells))
        east_level = lax.dynamic_index_in_dim(east_velocity, k, 0, keepdims=False).astype(jnp.float32)
        north_level = lax.dynamic_index_in_dim(north_velocity, k, 0, keepdims=False).astype(jnp.float32)
        stacked = jnp.concatenate([tracer_level, wet_level[None], east_level[None], north_level[None]], axis=0)
        return baroclinic(fold_pad(stacked, 2, fold_signs)), wet_level

    provisional, wet_mask = lax.map(level_update, jnp.arange(LEV, dtype=jnp.int32))
    provisional = jnp.moveaxis(provisional, 0, 1)
    new_tracers = vertical_mix(provisional, wet_mask, vertical_diffusivity.astype(jnp.float32))
    wet_surface = wet_mask[0]
    surface_source = wet_surface * (forcing + jnp.mean(new_tracers[0] - new_tracers[1], axis=0))
    centre_weight = 6.0 + surface_coupling

    def apply_operator(surface_field):
        return nine_point(fold_pad(surface_field, 1, 1.0), wet_surface, centre_weight)

    solution = jnp.zeros_like(surface_source)
    residual = surface_source
    precond = wet_surface * residual / centre_weight
    direction = precond
    resid_dot = jnp.sum(residual * precond)
    for iteration in range(ITERS):
        operator_image = apply_operator(direction)
        step_size = resid_dot / jnp.sum(direction * operator_image)
        solution = solution + step_size * direction
        if iteration + 1 < ITERS:
            residual = residual - step_size * operator_image
            precond = wet_surface * residual / centre_weight
            dot_next = jnp.sum(residual * precond)
            direction = precond + (dot_next / resid_dot) * direction
            resid_dot = dot_next
    return new_tracers, solution
```

```python
import functools

import jax
import jax.numpy as jnp
from jax import lax
from jax.experimental import pallas as pl
from jax.experimental.pallas import tpu as pltpu
from jax.sharding import PartitionSpec as P

F32 = jnp.float32
MESH = pl.DeviceIdType.MESH
VMEM = pl.BlockSpec(memory_space=pltpu.VMEM)
ANY = pl.BlockSpec(memory_space=pl.ANY)
PAD = 8
TILE = 128


def lane_index(shape):
    return lax.broadcasted_iota(jnp.int32, shape, len(shape) - 1)


def flip_tile(value):
    lane = lane_index(value.shape)
    for bit in range(7):
        step = 1 << bit
        value = jnp.where(
            lane & step != 0, pltpu.roll(value, step, 1), pltpu.roll(value, TILE - step, 1)
        )
    return value


def flip_row(value):
    tiles = value.shape[1] // TILE
    return jnp.concatenate(
        [flip_tile(value[:, t * TILE : (t + 1) * TILE]) for t in reversed(range(tiles))], axis=1
    )


def shift_lanes(value, by):
    width = value.shape[1]
    by = by % width
    return value if by == 0 else pltpu.roll(value, by, 1)


class Layout:
    def __init__(self, levels):
        self.levels = levels
        self.speed = 4 * levels
        self.depth = 5 * levels
        self.weight = 5 * levels + 3
        self.count = 5 * levels + 6
        self.rows = -(-self.count // 8) * 8


def copy_to(src, dst, send, recv, lon, lat):
    return pltpu.make_async_remote_copy(
        src_ref=src,
        dst_ref=dst,
        send_sem=send,
        recv_sem=recv,
        device_id={"lon": lon, "lat": lat},
        device_id_type=MESH,
    )


def greet(barrier, lon, lat):
    pl.semaphore_signal(barrier, inc=1, device_id={"lon": lon, "lat": lat}, device_id_type=MESH)


def ghost_kernel(
    lons, lats, levels,
    tr_ref, u_ref, v_ref, lev_ref, cw_ref,
    g_out, rs_out, rn_out,
    t_w, t_e, t_s, t_n, u_w, u_e, v_s, v_n,
    p_w, p_e, r_s, r_n, c_s, c_n, g_in, rs_in, rn_in,
    local_sem, send_sem, recv_sem,
):
    lay = Layout(levels)
    lon, lat = lax.axis_index("lon"), lax.axis_index("lat")
    rows, cols = lev_ref.shape
    east, west = lax.rem(lon + 1, lons), lax.rem(lon + lons - 1, lons)
    mirror = lons - 1 - lon
    top = lat == lats - 1
    bottom = lat == 0
    locals_ = [
        pltpu.make_async_copy(src, dst, local_sem.at[i])
        for i, (src, dst) in enumerate(
            (
                (tr_ref.at[:, :, 0:8, :], t_s),
                (tr_ref.at[:, :, rows - 8 : rows, :], t_n),
                (v_ref.at[:, 0:16, :], v_s),
                (v_ref.at[:, rows - 16 : rows, :], v_n),
                (tr_ref.at[:, :, :, 0:TILE], t_w),
                (tr_ref.at[:, :, :, cols - TILE : cols], t_e),
                (u_ref.at[:, :, 0:TILE], u_w),
                (u_ref.at[:, :, cols - TILE : cols], u_e),
            )
        )
    ]
    for copy in locals_:
        copy.start()
    barrier = pltpu.get_barrier_semaphore()
    greet(barrier, east, lat)
    greet(barrier, west, lat)

    @pl.when(top)
    def _():
        greet(barrier, mirror, lat)

    @pl.when(jnp.logical_not(top))
    def _():
        greet(barrier, lon, lat + 1)

    @pl.when(jnp.logical_not(bottom))
    def _():
        greet(barrier, lon, lat - 1)
        pl.semaphore_wait(barrier, 4)

    @pl.when(bottom)
    def _():
        pl.semaphore_wait(barrier, 3)
        rs_in[...] = jnp.zeros_like(rs_in)
        g_in[:, 0:PAD, :] = jnp.zeros_like(g_in[:, 0:PAD, :])

    for copy in locals_[0:4]:
        copy.wait()
    tail = 8 * (lay.depth // 8)
    r_s[tail:, :] = jnp.zeros_like(r_s[tail:, :])
    r_n[tail:, :] = jnp.zeros_like(r_n[tail:, :])
    for a in range(2):
        for k in range(levels):
            s = 2 * (a * levels + k)
            r_s[s : s + 2, :] = t_s[a, k, 0:2, :]
    for k in range(levels):
        r_s[lay.speed + k : lay.speed + k + 1, :] = v_s[k].astype(F32)[0:1, :]
    r_s[lay.depth : lay.depth + 3, :] = lev_ref[0:3, :]
    r_s[lay.weight : lay.weight + 3, :] = cw_ref[0:3, :]

    @pl.when(jnp.logical_not(top))
    def _():
        for a in range(2):
            for k in range(levels):
                s = 2 * (a * levels + k)
                r_n[s : s + 2, :] = t_n[a, k, 6:8, :]
        for k in range(levels):
            r_n[lay.speed + k : lay.speed + k + 1, :] = v_n[k].astype(F32)[15:16, :]
        r_n[lay.depth : lay.depth + 3, :] = lev_ref[rows - 3 : rows, :]
        r_n[lay.weight : lay.weight + 3, :] = cw_ref[rows - 3 : rows, :]

    @pl.when(top)
    def _():
        for a in range(2):
            for k in range(levels):
                s = 2 * (a * levels + k)
                r_n[s : s + 1, :] = t_n[a, k, 7:8, :]
                r_n[s + 1 : s + 2, :] = t_n[a, k, 6:7, :]
        for k in range(levels):
            r_n[lay.speed + k : lay.speed + k + 1, :] = -v_n[k].astype(F32)[15:16, :]
        for j in range(3):
            r_n[lay.depth + j : lay.depth + j + 1, :] = lev_ref[rows - 1 - j : rows - j, :]
            r_n[lay.weight + j : lay.weight + j + 1, :] = cw_ref[rows - 1 - j : rows - j, :]
        r_n[...] = flip_row(r_n[...])

    north_far = copy_to(r_n, rn_in, send_sem.at[0], recv_sem.at[0], mirror, lat)
    north_near = copy_to(r_n, rs_in, send_sem.at[0], recv_sem.at[1], lon, lat + 1)
    south = copy_to(r_s, rn_in, send_sem.at[1], recv_sem.at[0], lon, lat - 1)
    pl.when(top)(north_far.start)
    pl.when(jnp.logical_not(top))(north_near.start)
    pl.when(jnp.logical_not(bottom))(south.start)

    for copy in locals_[4:]:
        copy.wait()
    lane = lane_index((rows, TILE))
    back = TILE - 1 - lane
    first, last = jnp.zeros((rows, TILE), F32), jnp.zeros((rows, TILE), F32)
    for a in range(2):
        for k in range(levels):
            s = 2 * (a * levels + k)
            first = jnp.where(lane >> 1 == s // 2, shift_lanes(t_w[a, k], s), first)
            last = jnp.where(back >> 1 == s // 2, shift_lanes(t_e[a, k], -s), last)
    for k in range(levels):
        s = lay.speed + k
        first = jnp.where(lane == s, shift_lanes(u_w[k].astype(F32), s), first)
        last = jnp.where(back == s, shift_lanes(u_e[k].astype(F32), -s), last)
    for ref, s in ((lev_ref, lay.depth), (cw_ref, lay.weight)):
        inside = jnp.logical_and(lane >= s, lane < s + 3)
        first = jnp.where(inside, shift_lanes(ref[:, 0:TILE], s), first)
        inside = jnp.logical_and(back >= s, back < s + 3)
        last = jnp.where(inside, shift_lanes(ref[:, cols - TILE : cols], -s), last)
    p_w[...] = first
    p_e[...] = last
    own = slice(PAD, PAD + rows)
    to_west = copy_to(p_w, g_in.at[1, own, :], send_sem.at[2], recv_sem.at[2], west, lat)
    to_east = copy_to(p_e, g_in.at[0, own, :], send_sem.at[3], recv_sem.at[3], east, lat)
    to_west.start()
    to_east.start()
    to_west.wait_recv()
    to_east.wait_recv()
    c_s[...] = g_in[:, PAD : 2 * PAD, :]

    @pl.when(jnp.logical_not(top))
    def _():
        c_n[...] = g_in[:, rows : rows + PAD, :]

    @pl.when(top)
    def _():
        for side in range(2):
            turned = flip_tile(g_in[1 - side, rows : rows + PAD, :])
            for j in range(PAD):
                c_n[side, j : j + 1, :] = turned[PAD - 1 - j : PAD - j, :]

    high = g_in.at[:, PAD + rows : 2 * PAD + rows, :]
    low = g_in.at[:, 0:PAD, :]
    corner_far = copy_to(c_n, high, send_sem.at[4], recv_sem.at[4], mirror, lat)
    corner_near = copy_to(c_n, low, send_sem.at[4], recv_sem.at[5], lon, lat + 1)
    corner_south = copy_to(c_s, high, send_sem.at[5], recv_sem.at[4], lon, lat - 1)
    pl.when(top)(corner_far.start)
    pl.when(jnp.logical_not(top))(corner_near.start)
    pl.when(jnp.logical_not(bottom))(corner_south.start)

    north_far.wait_recv()
    rn_out[...] = rn_in[...]
    pl.when(jnp.logical_not(bottom))(north_near.wait_recv)
    rs_out[...] = rs_in[...]
    corner_far.wait_recv()
    pl.when(jnp.logical_not(bottom))(corner_near.wait_recv)
    g_out[...] = g_in[...]
    north_far.wait_send()
    corner_far.wait_send()
    to_west.wait_send()
    to_east.wait_send()
    pl.when(jnp.logical_not(bottom))(south.wait_send)
    pl.when(jnp.logical_not(bottom))(corner_south.wait_send)


def unpacked(g_ref, slot):
    lane = lane_index(g_ref.shape[1:])
    return jnp.where(
        lane < TILE // 2,
        pltpu.roll(g_ref[1], TILE - slot, 1),
        pltpu.roll(g_ref[0], slot, 1),
    )


def column_kernel(
    levels,
    tr_ref, u_ref, v_ref, kd_ref, lev_ref, forcing_ref, g_ref, rs_ref, rn_ref,
    out_ref, src_ref,
    tr, u, v, kd, vx, ux, lv, mk, q, lap, sm, ratio, red, coup,
    in_sem, out_sem,
):
    lay = Layout(levels)
    rows, cols = lev_ref.shape
    own = slice(PAD, PAD + rows)
    ghost = slice(cols, cols + TILE)

    def inputs(k):
        return (
            pltpu.make_async_copy(tr_ref.at[:, k], tr.at[:, k, own, 0:cols], in_sem.at[0, k]),
            pltpu.make_async_copy(u_ref.at[k], u.at[k], in_sem.at[1, k]),
            pltpu.make_async_copy(v_ref.at[k], v.at[k], in_sem.at[2, k]),
            pltpu.make_async_copy(kd_ref.at[k], kd.at[k], in_sem.at[3, k]),
        )

    def outputs(k):
        return pltpu.make_async_copy(red.at[:, k + 1], out_ref.at[:, k], out_sem.at[k])

    for k in range(levels):
        for copy in inputs(k):
            copy.start()
    for k in range(levels):
        for a in range(2):
            s = 2 * (a * levels + k)
            tr[a, k, PAD - 2 : PAD, 0:cols] = rs_ref[s : s + 2, :]
            tr[a, k, PAD + rows : PAD + rows + 2, 0:cols] = rn_ref[s : s + 2, :]
        s = lay.speed + k
        vx[k, PAD - 1 : PAD, :] = rs_ref[s : s + 1, :]
        vx[k, PAD + rows : PAD + rows + 1, :] = rn_ref[s : s + 1, :]
    lv[...] = jnp.zeros_like(lv)
    lv[own, 0:cols] = lev_ref[...]
    lv[PAD - 3 : PAD, 0:cols] = rs_ref[lay.depth : lay.depth + 3, :]
    lv[PAD + rows : PAD + rows + 3, 0:cols] = rn_ref[lay.depth : lay.depth + 3, :]
    lv[:, ghost] = unpacked(g_ref, lay.depth)
    coup[...] = jnp.zeros_like(coup)
    ratio[0] = jnp.zeros_like(ratio[0])
    red[:, 0] = jnp.zeros_like(red[:, 0])
    width = cols + TILE

    def right(value):
        return pltpu.roll(value, width - 1, 1)

    def left(value):
        return pltpu.roll(value, 1, 1)

    for copy in inputs(0):
        copy.wait()

    def down(k, carry):
        later = jnp.minimum(k + 1, levels - 1)

        @pl.when(k + 1 < levels)
        def _():
            for copy in inputs(later):
                copy.wait()

        level = k.astype(F32)
        ux[:, 0:cols] = u[k].astype(F32)
        ux[:, ghost] = unpacked(g_ref, lay.speed + k)[own]
        vx[k, own, :] = v[k].astype(F32)
        for a in range(2):
            tr[a, k, :, ghost] = unpacked(g_ref, 2 * (a * levels + k))
        for c in range(0, rows + 2 * PAD, 8):
            here = slice(c, c + 8)
            wet = jnp.where(lv[here] > level, 1.0, 0.0)
            mk[here] = wet
            for a in range(2):
                q[a, here] = wet * tr[a, k, here]
        for c in range(0, rows + 8, 8):
            base = c + PAD - 1
            wet = mk[base : base + 8]
            total = right(wet) + left(wet) + mk[base - 1 : base + 7] + mk[base + 1 : base + 9]
            sm[c : c + 8] = total
            for a in range(2):
                mid = q[a, base : base + 8]
                around = right(mid) + left(mid) + q[a, base - 1 : base + 7] + q[a, base + 1 : base + 9]
                lap[a, c : c + 8] = wet * (around - mid * total)
        for c in range(0, rows, 8):
            base = c + PAD
            here = slice(c, c + 8)
            wet_wide = mk[base : base + 8]
            wet = wet_wide[:, 0:cols]
            speed = ux[here]
            face = 0.25 * (speed + right(speed)) * (wet_wide * right(wet_wide))
            u_west = left(face)[:, 0:cols]
            u_east = face[:, 0:cols]
            v_mid = vx[k, base : base + 8]
            v_north = 0.25 * (v_mid + vx[k, base + 1 : base + 9]) * (wet * mk[base + 1 : base + 9, 0:cols])
            v_south = 0.25 * (v_mid + vx[k, base - 1 : base + 7]) * (wet * mk[base - 1 : base + 7, 0:cols])
            spread = u_east - u_west + v_north - v_south
            total = sm[c + 1 : c + 9, 0:cols]
            above = coup[here]
            below = kd[later, here].astype(F32) * jnp.where(lv[base : base + 8, 0:cols] > level + 1.0, 1.0, 0.0)
            inverse = 1.0 / (1.0 + above + below + above * ratio[k, here])
            ratio[k + 1, here] = -below * inverse
            coup[here] = below
            for a in range(2):
                wide = q[a, base : base + 8]
                mid = wide[:, 0:cols]
                divergence = (
                    mid * spread
                    + u_east * right(wide)[:, 0:cols]
                    - u_west * left(wide)[:, 0:cols]
                    + v_north * q[a, base + 1 : base + 9, 0:cols]
                    - v_south * q[a, base - 1 : base + 7, 0:cols]
                )
                lap_wide = lap[a, c + 1 : c + 9]
                around = (
                    right(lap_wide)[:, 0:cols]
                    + left(lap_wide)[:, 0:cols]
                    + lap[a, c + 2 : c + 10, 0:cols]
                    + lap[a, c : c + 8, 0:cols]
                )
                lap_two = wet * (around - lap_wide[:, 0:cols] * total)
                value = mid - 0.25 * divergence - 0.01 * lap_two
                red[a, k + 1, here] = (value + above * red[a, k, here]) * inverse
        return carry

    lax.fori_loop(0, levels, down, 0)
    outputs(levels - 1).start()
    coup[...] = red[0, levels] - red[1, levels]

    def up(i, carry):
        k = levels - 2 - i
        for c in range(0, rows, 8):
            here = slice(c, c + 8)
            factor = ratio[k + 1, here]
            one = red[0, k + 1, here] - factor * red[0, k + 2, here]
            two = red[1, k + 1, here] - factor * red[1, k + 2, here]
            red[0, k + 1, here] = one
            red[1, k + 1, here] = two
            coup[here] = coup[here] + (one - two)
        outputs(k).start()
        return carry

    lax.fori_loop(0, levels - 1, up, 0)
    src_ref[...] = jnp.where(
        lev_ref[...] > 0.0, forcing_ref[...] + coup[...] * (1.0 / levels), 0.0
    )
    for k in range(levels):
        outputs(k).wait()


def solve_kernel(
    lons, lats, levels,
    src_ref, lev_ref, cw_ref, g_ref, rs_ref, rn_ref,
    out_ref,
    lv, cw, bx, side_in, row_n, row_in, corner, corner_in, part, lon_in, joint, lat_in,
    send_sem, recv_sem, lon_send, lon_recv, lat_send, lat_recv,
):
    lay = Layout(levels)
    rows, cols = src_ref.shape
    lon, lat = lax.axis_index("lon"), lax.axis_index("lat")
    east, west = lax.rem(lon + 1, lons), lax.rem(lon + lons - 1, lons)
    mirror = lons - 1 - lon
    top = lat == lats - 1
    bottom = lat == 0
    own = slice(PAD, PAD + rows)
    north_rows = slice(PAD + rows, 2 * PAD + rows)
    ghost = slice(cols, cols + TILE)
    lon_peers = [lax.rem(lon + d, lons) for d in range(1, lons)]
    lat_peers = [lax.rem(lat + d, lats) for d in range(1, lats)]
    barrier = pltpu.get_barrier_semaphore()
    for peer in lon_peers:
        greet(barrier, peer, lat)
    for peer in lat_peers:
        greet(barrier, lon, peer)

    @pl.when(jnp.logical_not(top))
    def _():
        row_n[...] = src_ref[rows - 8 : rows, :]

    @pl.when(top)
    def _():
        turned = flip_row(src_ref[rows - 8 : rows, :])
        for j in range(8):
            row_n[j : j + 1, :] = turned[7 - j : 8 - j, :]

    @pl.when(bottom)
    def _():
        row_in[0] = jnp.zeros_like(row_in[0])
        corner_in[0] = jnp.zeros_like(corner_in[0])

    pl.semaphore_wait(barrier, lons - 1 + lats - 1)
    to_west = copy_to(src_ref.at[:, 0:TILE], side_in.at[1], send_sem.at[2], recv_sem.at[2], west, lat)
    to_east = copy_to(src_ref.at[:, cols - TILE : cols], side_in.at[0], send_sem.at[3], recv_sem.at[3], east, lat)
    to_west.start()
    to_east.start()
    north_far = copy_to(row_n, row_in.at[1], send_sem.at[0], recv_sem.at[0], mirror, lat)
    north_near = copy_to(row_n, row_in.at[0], send_sem.at[0], recv_sem.at[1], lon, lat + 1)
    south = copy_to(src_ref.at[0:8, :], row_in.at[1], send_sem.at[1], recv_sem.at[0], lon, lat - 1)
    pl.when(top)(north_far.start)
    pl.when(jnp.logical_not(top))(north_near.start)
    pl.when(jnp.logical_not(bottom))(south.start)

    for plane, own_ref, slot, empty in ((lv, lev_ref, lay.depth, 0.0), (cw, cw_ref, lay.weight, 1.0)):
        plane[...] = jnp.full(plane.shape, empty, F32)
        plane[own, 0:cols] = own_ref[...]
        plane[PAD - 3 : PAD, 0:cols] = rs_ref[slot : slot + 3, :]
        plane[PAD + rows : PAD + rows + 3, 0:cols] = rn_ref[slot : slot + 3, :]
        plane[:, ghost] = unpacked(g_ref, slot)
    wet = lv[...] > 0.0
    cw[...] = jnp.where(wet, cw[...], 1.0)
    lv[...] = jnp.where(wet, 1.0 / cw[...], 0.0)
    bx[own, 0:cols] = src_ref[...]

    to_west.wait_recv()
    to_east.wait_recv()
    lane = lane_index((rows, TILE))
    bx[own, ghost] = jnp.where(lane < TILE // 2, side_in[1], side_in[0])
    lane = lane_index((8, TILE))
    edge = bx[rows : rows + 8, ghost]
    corner[1] = bx[PAD : PAD + 8, ghost]

    @pl.when(jnp.logical_not(top))
    def _():
        corner[0] = edge

    @pl.when(top)
    def _():
        turned = flip_tile(edge)
        for j in range(8):
            corner[0, j : j + 1, :] = turned[7 - j : 8 - j, :]

    corner_far = copy_to(corner.at[0], corner_in.at[1], send_sem.at[4], recv_sem.at[4], mirror, lat)
    corner_near = copy_to(corner.at[0], corner_in.at[0], send_sem.at[4], recv_sem.at[5], lon, lat + 1)
    corner_south = copy_to(corner.at[1], corner_in.at[1], send_sem.at[5], recv_sem.at[4], lon, lat - 1)
    pl.when(top)(corner_far.start)
    pl.when(jnp.logical_not(top))(corner_near.start)
    pl.when(jnp.logical_not(bottom))(corner_south.start)
    north_far.wait_recv()
    bx[north_rows, 0:cols] = row_in[1]
    pl.when(jnp.logical_not(bottom))(north_near.wait_recv)
    bx[0:PAD, 0:cols] = row_in[0]
    corner_far.wait_recv()
    bx[north_rows, ghost] = corner_in[1]
    pl.when(jnp.logical_not(bottom))(corner_near.wait_recv)
    bx[0:PAD, ghost] = corner_in[0]

    height, width = bx.shape

    def operator(field):
        sides = pltpu.roll(field, 1, 1) + pltpu.roll(field, width - 1, 1)
        triple = field + 0.5 * sides
        ends = pltpu.roll(triple, 1, 0) + pltpu.roll(triple, height - 1, 0)
        return cw[...] * field - sides - ends

    zero = lv[...] * bx[...]
    image_zero = operator(zero)
    one = lv[...] * image_zero - zero
    image_one = operator(one)
    two = 2.0 * (lv[...] * image_one - one) - zero
    image_two = operator(two)

    def inner(value):
        return value[own, 0:cols]

    base = [inner(zero), inner(one), inner(two)]
    images = [inner(image_zero), inner(image_one), inner(image_two)]
    source = src_ref[...]
    pairs = [
        (base[0], images[0]), (base[1], images[0]), (base[2], images[0]),
        (base[1], images[1]), (base[2], images[1]), (base[2], images[2]),
        (base[0], source), (base[1], source), (base[2], source),
    ]
    part[8:16, :] = jnp.zeros((8, TILE), F32)
    for i, (x, y) in enumerate(pairs):
        line = jnp.sum(x * y, axis=0, keepdims=True)
        part[i : i + 1, :] = sum(line[:, t : t + TILE] for t in range(0, cols, TILE))
    over_lon = [
        copy_to(part, lon_in.at[d], lon_send.at[d], lon_recv.at[d], peer, lat)
        for d, peer in enumerate(lon_peers)
    ]
    for copy in over_lon:
        copy.start()
    for copy in over_lon:
        copy.wait_recv()
    joint[...] = part[...] + jnp.sum(lon_in[...], axis=0)
    over_lat = [
        copy_to(joint, lat_in.at[d], lat_send.at[d], lat_recv.at[d], lon, peer)
        for d, peer in enumerate(lat_peers)
    ]
    for copy in over_lat:
        copy.start()
    for copy in over_lat:
        copy.wait_recv()
    totals = jnp.sum(joint[...] + jnp.sum(lat_in[...], axis=0), axis=1, keepdims=True)
    g00, g01, g02, g11, g12, g22, d0, d1, d2 = (totals[i : i + 1, :] for i in range(9))
    small = 1e-9 * g00
    l10, l20 = g01 / g00, g02 / g00
    pivot_one = g11 - l10 * g01
    inverse_one = jnp.where(pivot_one > small, 1.0 / pivot_one, 0.0)
    cross = g12 - l20 * g01
    l21 = cross * inverse_one
    pivot_two = g22 - l20 * g02 - l21 * cross
    inverse_two = jnp.where(pivot_two > small, 1.0 / pivot_two, 0.0)
    y1 = d1 - l10 * d0
    y2 = d2 - l20 * d0 - l21 * y1
    c2 = y2 * inverse_two
    c1 = y1 * inverse_one - l21 * c2
    c0 = d0 / g00 - l10 * c1 - l20 * c2
    out_ref[...] = c0 * base[0] + c1 * base[1] + c2 * base[2]

    to_west.wait_send()
    to_east.wait_send()
    north_far.wait_send()
    corner_far.wait_send()
    pl.when(jnp.logical_not(bottom))(south.wait_send)
    pl.when(jnp.logical_not(bottom))(corner_south.wait_send)
    for copy in over_lon + over_lat:
        copy.wait_send()


def shards(
    lons, lats,
    tracers, east_velocity, north_velocity, vertical_diffusivity,
    depth_levels, ocean_blocks, forcing, surface_coupling,
):
    levels, rows, cols = tracers.shape[1:]
    lay = Layout(levels)
    ocean_cells = jnp.repeat(
        jnp.repeat(ocean_blocks, rows // ocean_blocks.shape[0], axis=0),
        cols // ocean_blocks.shape[1],
        axis=1,
    )
    depth = jnp.where(ocean_cells > 0, depth_levels, 0).astype(F32)
    weight = 6.0 + surface_coupling
    high, wide = rows + 2 * PAD, cols + TILE
    dma = pltpu.SemaphoreType.DMA
    strip = jax.ShapeDtypeStruct((lay.rows, cols), F32)
    bf16 = jnp.bfloat16
    ghosts, south, north = pl.pallas_call(
        functools.partial(ghost_kernel, lons, lats, levels),
        out_shape=(jax.ShapeDtypeStruct((2, high, TILE), F32), strip, strip),
        in_specs=[ANY, ANY, ANY, VMEM, VMEM],
        out_specs=(VMEM, VMEM, VMEM),
        scratch_shapes=[
            pltpu.VMEM((2, levels, rows, TILE), F32),
            pltpu.VMEM((2, levels, rows, TILE), F32),
            pltpu.VMEM((2, levels, 8, cols), F32),
            pltpu.VMEM((2, levels, 8, cols), F32),
            pltpu.VMEM((levels, rows, TILE), bf16),
            pltpu.VMEM((levels, rows, TILE), bf16),
            pltpu.VMEM((levels, 16, cols), bf16),
            pltpu.VMEM((levels, 16, cols), bf16),
            pltpu.VMEM((rows, TILE), F32),
            pltpu.VMEM((rows, TILE), F32),
            pltpu.VMEM((lay.rows, cols), F32),
            pltpu.VMEM((lay.rows, cols), F32),
            pltpu.VMEM((2, PAD, TILE), F32),
            pltpu.VMEM((2, PAD, TILE), F32),
            pltpu.VMEM((2, high, TILE), F32),
            pltpu.VMEM((lay.rows, cols), F32),
            pltpu.VMEM((lay.rows, cols), F32),
            dma((8,)), dma((6,)), dma((6,)),
        ],
        compiler_params=pltpu.CompilerParams(
            collective_id=0, has_side_effects=True, vmem_limit_bytes=32 << 20
        ),
        name="ghosts",
    )(tracers, east_velocity, north_velocity, depth, weight)
    new_tracers, source = pl.pallas_call(
        functools.partial(column_kernel, levels),
        out_shape=(
            jax.ShapeDtypeStruct(tracers.shape, F32),
            jax.ShapeDtypeStruct((rows, cols), F32),
        ),
        in_specs=[ANY] * 4 + [VMEM] * 5,
        out_specs=(ANY, VMEM),
        scratch_shapes=[
            pltpu.VMEM((2, levels, high, wide), F32),
            pltpu.VMEM((levels, rows, cols), bf16),
            pltpu.VMEM((levels, rows, cols), bf16),
            pltpu.VMEM((levels, rows, cols), bf16),
            pltpu.VMEM((levels, high, cols), F32),
            pltpu.VMEM((rows, wide), F32),
            pltpu.VMEM((high, wide), F32),
            pltpu.VMEM((high, wide), F32),
            pltpu.VMEM((2, high, wide), F32),
            pltpu.VMEM((2, high, wide), F32),
            pltpu.VMEM((high, wide), F32),
            pltpu.VMEM((levels + 1, rows, cols), F32),
            pltpu.VMEM((2, levels + 1, rows, cols), F32),
            pltpu.VMEM((rows, cols), F32),
            dma((4, levels)), dma((levels,)),
        ],
        compiler_params=pltpu.CompilerParams(vmem_limit_bytes=48 << 20),
        name="columns",
    )(tracers, east_velocity, north_velocity, vertical_diffusivity, depth, forcing, ghosts, south, north)
    surface = pl.pallas_call(
        functools.partial(solve_kernel, lons, lats, levels),
        out_shape=jax.ShapeDtypeStruct((rows, cols), F32),
        in_specs=[VMEM] * 6,
        out_specs=VMEM,
        scratch_shapes=[
            pltpu.VMEM((high, wide), F32),
            pltpu.VMEM((high, wide), F32),
            pltpu.VMEM((high, wide), F32),
            pltpu.VMEM((2, rows, TILE), F32),
            pltpu.VMEM((8, cols), F32),
            pltpu.VMEM((2, 8, cols), F32),
            pltpu.VMEM((2, 8, TILE), F32),
            pltpu.VMEM((2, 8, TILE), F32),
            pltpu.VMEM((16, TILE), F32),
            pltpu.VMEM((lons - 1, 16, TILE), F32),
            pltpu.VMEM((16, TILE), F32),
            pltpu.VMEM((lats - 1, 16, TILE), F32),
            dma((6,)), dma((6,)),
            dma((lons - 1,)), dma((lons - 1,)), dma((lats - 1,)), dma((lats - 1,)),
        ],
        compiler_params=pltpu.CompilerParams(
            collective_id=1, has_side_effects=True, vmem_limit_bytes=32 << 20
        ),
        name="surface",
    )(source, depth, weight, ghosts, south, north)
    return new_tracers, surface


def solution(mesh):
    flat = P("lat", "lon")
    deep = P(None, "lat", "lon")
    tracer = P(None, None, "lat", "lon")
    return jax.shard_map(
        functools.partial(shards, mesh.shape["lon"], mesh.shape["lat"]),
        mesh=mesh,
        in_specs=(tracer, deep, deep, deep, flat, flat, flat, flat),
        out_specs=(tracer, flat),
        check_vma=False,
    )
```

```python
import functools

import jax
import jax.numpy as jnp
from jax import lax
from jax.experimental import pallas as pl
from jax.experimental.pallas import tpu as pltpu
from jax.sharding import PartitionSpec as P

F32 = jnp.float32
MESH = pl.DeviceIdType.MESH
VMEM = pl.BlockSpec(memory_space=pltpu.VMEM)
HBM = pl.BlockSpec(memory_space=pltpu.HBM)
PAD = 8
TILE = 128


def lane_index(shape):
    return lax.broadcasted_iota(jnp.int32, shape, len(shape) - 1)


def flip_tile(value):
    lane = lane_index(value.shape)
    for bit in range(7):
        step = 1 << bit
        value = jnp.where(
            lane & step != 0, pltpu.roll(value, step, 1), pltpu.roll(value, TILE - step, 1)
        )
    return value


def flip_row(value):
    tiles = value.shape[1] // TILE
    return jnp.concatenate(
        [flip_tile(value[:, t * TILE : (t + 1) * TILE]) for t in reversed(range(tiles))], axis=1
    )


def shift_lanes(value, by):
    width = value.shape[1]
    by = by % width
    return value if by == 0 else pltpu.roll(value, by, 1)


class Layout:
    def __init__(self, levels):
        self.levels = levels
        self.speed = 4 * levels
        self.depth = 5 * levels
        self.weight = 5 * levels + 3
        self.count = 5 * levels + 6
        self.rows = -(-self.count // 8) * 8


def copy_to(src, dst, send, recv, lon, lat):
    return pltpu.make_async_remote_copy(
        src_ref=src,
        dst_ref=dst,
        send_sem=send,
        recv_sem=recv,
        device_id={"lon": lon, "lat": lat},
        device_id_type=MESH,
    )


def greet(barrier, lon, lat):
    pl.semaphore_signal(barrier, inc=1, device_id={"lon": lon, "lat": lat}, device_id_type=MESH)


class Corners:
    def __init__(self, lons, lats, sources, turned, dst, send, recv):
        lon, lat = lax.axis_index("lon"), lax.axis_index("lat")
        east, west = lax.rem(lon + 1, lons), lax.rem(lon + lons - 1, lons)
        self.top, self.bottom = lat == lats - 1, lat == 0
        far_first, far_last = lax.rem(lons - lon, lons), lax.rem(2 * lons - 2 - lon, lons)
        self.own_first = jnp.logical_and(self.top, far_first == lon)
        self.own_last = jnp.logical_and(self.top, far_last == lon)
        self.turned, self.dst = turned, dst
        high_first, high_last, low_first, low_last = sources
        turned_first, turned_last = turned
        self.up_last = copy_to(high_last, dst.at[0, 0], send.at[0], recv.at[0], east, lat + 1)
        self.up_first = copy_to(high_first, dst.at[0, 1], send.at[1], recv.at[1], west, lat + 1)
        self.far_first = copy_to(turned_first, dst.at[1, 0], send.at[1], recv.at[2], far_first, lat)
        self.far_last = copy_to(turned_last, dst.at[1, 1], send.at[0], recv.at[3], far_last, lat)
        self.down_last = copy_to(low_last, dst.at[1, 0], send.at[2], recv.at[2], east, lat - 1)
        self.down_first = copy_to(low_first, dst.at[1, 1], send.at[3], recv.at[3], west, lat - 1)

    def start(self):
        @pl.when(jnp.logical_not(self.top))
        def _():
            self.up_last.start()
            self.up_first.start()

        @pl.when(jnp.logical_not(self.bottom))
        def _():
            self.down_last.start()
            self.down_first.start()

        pl.when(jnp.logical_and(self.top, jnp.logical_not(self.own_first)))(self.far_first.start)
        pl.when(jnp.logical_and(self.top, jnp.logical_not(self.own_last)))(self.far_last.start)

        @pl.when(self.own_first)
        def _():
            self.dst[1, 0] = self.turned[0][...]

        @pl.when(self.own_last)
        def _():
            self.dst[1, 1] = self.turned[1][...]

        @pl.when(self.bottom)
        def _():
            self.dst[0] = jnp.zeros_like(self.dst[0])

    def wait_recv(self):
        @pl.when(jnp.logical_not(self.bottom))
        def _():
            self.up_last.wait_recv()
            self.up_first.wait_recv()

        pl.when(jnp.logical_not(self.own_first))(self.far_first.wait_recv)
        pl.when(jnp.logical_not(self.own_last))(self.far_last.wait_recv)

    def wait_send(self):
        pl.when(jnp.logical_not(self.own_last))(self.up_last.wait_send)
        pl.when(jnp.logical_not(self.own_first))(self.up_first.wait_send)

        @pl.when(jnp.logical_not(self.bottom))
        def _():
            self.down_last.wait_send()
            self.down_first.wait_send()


def ghost_kernel(
    lons, lats, levels,
    tr_ref, u_ref, v_ref, depth_ref, ocean_ref, coupling_ref,
    g_out, rs_out, rn_out, lev_ref, cw_ref,
    t_w, t_e, t_s, t_n, u_w, u_e, v_s, v_n,
    p_w, p_e, r_s, r_n, turned, corner_in, g_in, rs_in, rn_in,
    local_sem, send_sem, recv_sem, corner_send, corner_recv,
):
    lay = Layout(levels)
    lon, lat = lax.axis_index("lon"), lax.axis_index("lat")
    rows, cols = depth_ref.shape
    east, west = lax.rem(lon + 1, lons), lax.rem(lon + lons - 1, lons)
    mirror = lons - 1 - lon
    top = lat == lats - 1
    bottom = lat == 0
    locals_ = [
        pltpu.make_async_copy(src, dst, local_sem.at[i])
        for i, (src, dst) in enumerate(
            (
                (tr_ref.at[:, :, 0:8, :], t_s),
                (tr_ref.at[:, :, rows - 8 : rows, :], t_n),
                (v_ref.at[:, 0:16, :], v_s),
                (v_ref.at[:, rows - 16 : rows, :], v_n),
                (tr_ref.at[:, :, :, 0:TILE], t_w),
                (tr_ref.at[:, :, :, cols - TILE : cols], t_e),
                (u_ref.at[:, :, 0:TILE], u_w),
                (u_ref.at[:, :, cols - TILE : cols], u_e),
            )
        )
    ]
    for copy in locals_:
        copy.start()
    barrier = pltpu.get_barrier_semaphore()
    greet(barrier, east, lat)
    greet(barrier, west, lat)

    @pl.when(top)
    def _():
        greet(barrier, mirror, lat)

        greet(barrier, lax.rem(lons - lon, lons), lat)
        greet(barrier, lax.rem(2 * lons - 2 - lon, lons), lat)

    @pl.when(jnp.logical_not(top))
    def _():
        for peer in (lon, east, west):
            greet(barrier, peer, lat + 1)

    @pl.when(jnp.logical_not(bottom))
    def _():
        for peer in (lon, east, west):
            greet(barrier, peer, lat - 1)

    @pl.when(bottom)
    def _():
        rs_in[...] = jnp.zeros_like(rs_in)

    row = lax.broadcasted_iota(jnp.int32, (rows, cols), 0)
    col = lane_index((rows, cols))
    tall, broad = rows // ocean_ref.shape[0], cols // ocean_ref.shape[1]
    cells = jnp.zeros((rows, cols), jnp.int32)
    for i in range(ocean_ref.shape[0]):
        for j in range(ocean_ref.shape[1]):
            inside = (row >= i * tall) & (row < (i + 1) * tall) & (col >= j * broad) & (col < (j + 1) * broad)
            cells = jnp.where(inside, ocean_ref[i, j], cells)
    lev_ref[...] = jnp.where(cells > 0, depth_ref[...], 0).astype(F32)
    cw_ref[...] = 6.0 + coupling_ref[...]
    for copy in locals_[0:4]:
        copy.wait()
    tail = 8 * (lay.depth // 8)
    r_s[tail:, :] = jnp.zeros_like(r_s[tail:, :])
    r_n[tail:, :] = jnp.zeros_like(r_n[tail:, :])
    for a in range(2):
        for k in range(levels):
            s = 2 * (a * levels + k)
            r_s[s : s + 2, :] = t_s[a, k, 0:2, :]
    for k in range(levels):
        r_s[lay.speed + k : lay.speed + k + 1, :] = v_s[k].astype(F32)[0:1, :]
    r_s[lay.depth : lay.depth + 3, :] = lev_ref[0:3, :]
    r_s[lay.weight : lay.weight + 3, :] = cw_ref[0:3, :]

    @pl.when(jnp.logical_not(top))
    def _():
        for a in range(2):
            for k in range(levels):
                s = 2 * (a * levels + k)
                r_n[s : s + 2, :] = t_n[a, k, 6:8, :]
        for k in range(levels):
            r_n[lay.speed + k : lay.speed + k + 1, :] = v_n[k].astype(F32)[15:16, :]
        r_n[lay.depth : lay.depth + 3, :] = lev_ref[rows - 3 : rows, :]
        r_n[lay.weight : lay.weight + 3, :] = cw_ref[rows - 3 : rows, :]

    @pl.when(top)
    def _():
        for a in range(2):
            for k in range(levels):
                s = 2 * (a * levels + k)
                r_n[s : s + 1, :] = t_n[a, k, 7:8, :]
                r_n[s + 1 : s + 2, :] = t_n[a, k, 6:7, :]
        for k in range(levels):
            r_n[lay.speed + k : lay.speed + k + 1, :] = -v_n[k].astype(F32)[15:16, :]
        for j in range(3):
            r_n[lay.depth + j : lay.depth + j + 1, :] = lev_ref[rows - 1 - j : rows - j, :]
            r_n[lay.weight + j : lay.weight + j + 1, :] = cw_ref[rows - 1 - j : rows - j, :]
        r_n[...] = flip_row(r_n[...])

    @pl.when(bottom)
    def _():
        pl.semaphore_wait(barrier, 5)

    @pl.when(top)
    def _():
        pl.semaphore_wait(barrier, 8)

    @pl.when(jnp.logical_not(jnp.logical_or(top, bottom)))
    def _():
        pl.semaphore_wait(barrier, 8)

    north_far = copy_to(r_n, rn_in, send_sem.at[0], recv_sem.at[0], mirror, lat)
    north_near = copy_to(r_n, rs_in, send_sem.at[0], recv_sem.at[1], lon, lat + 1)
    south = copy_to(r_s, rn_in, send_sem.at[1], recv_sem.at[0], lon, lat - 1)
    pl.when(top)(north_far.start)
    pl.when(jnp.logical_not(top))(north_near.start)
    pl.when(jnp.logical_not(bottom))(south.start)

    for copy in locals_[4:]:
        copy.wait()
    lane = lane_index((rows, TILE))
    back = TILE - 1 - lane
    first, last = jnp.zeros((rows, TILE), F32), jnp.zeros((rows, TILE), F32)
    for a in range(2):
        for k in range(levels):
            s = 2 * (a * levels + k)
            first = jnp.where(lane >> 1 == s // 2, shift_lanes(t_w[a, k], s), first)
            last = jnp.where(back >> 1 == s // 2, shift_lanes(t_e[a, k], -s), last)
    for k in range(levels):
        s = lay.speed + k
        first = jnp.where(lane == s, shift_lanes(u_w[k].astype(F32), s), first)
        last = jnp.where(back == s, shift_lanes(u_e[k].astype(F32), -s), last)
    for ref, s in ((lev_ref, lay.depth), (cw_ref, lay.weight)):
        inside = jnp.logical_and(lane >= s, lane < s + 3)
        first = jnp.where(inside, shift_lanes(ref[:, 0:TILE], s), first)
        inside = jnp.logical_and(back >= s, back < s + 3)
        last = jnp.where(inside, shift_lanes(ref[:, cols - TILE : cols], -s), last)
    p_w[...] = first
    p_e[...] = last
    own = slice(PAD, PAD + rows)
    to_west = copy_to(p_w, g_in.at[1], send_sem.at[2], recv_sem.at[2], west, lat)
    to_east = copy_to(p_e, g_in.at[0], send_sem.at[3], recv_sem.at[3], east, lat)
    to_west.start()
    to_east.start()

    @pl.when(top)
    def _():
        for side, value in enumerate((first, last)):
            back_tile = flip_tile(value[rows - PAD : rows, :])
            for j in range(PAD):
                turned[side, j : j + 1, :] = back_tile[PAD - 1 - j : PAD - j, :]

    corners = Corners(
        lons, lats,
        (p_w.at[rows - PAD : rows, :], p_e.at[rows - PAD : rows, :], p_w.at[0:PAD, :], p_e.at[0:PAD, :]),
        (turned.at[0], turned.at[1]),
        corner_in, corner_send, corner_recv,
    )
    corners.start()
    north_far.wait_recv()
    rn_out[...] = rn_in[...]
    pl.when(jnp.logical_not(bottom))(north_near.wait_recv)
    rs_out[...] = rs_in[...]
    to_west.wait_recv()
    to_east.wait_recv()
    g_out[:, own, :] = g_in[...]
    corners.wait_recv()
    g_out[:, 0:PAD, :] = corner_in[0]
    g_out[:, PAD + rows : 2 * PAD + rows, :] = corner_in[1]
    north_far.wait_send()
    to_west.wait_send()
    to_east.wait_send()
    pl.when(jnp.logical_not(bottom))(south.wait_send)
    corners.wait_send()


def unpacked(g_ref, slot):
    lane = lane_index(g_ref.shape[1:])
    return jnp.where(
        lane < TILE // 2,
        pltpu.roll(g_ref[1], TILE - slot, 1),
        pltpu.roll(g_ref[0], slot, 1),
    )


def column_kernel(
    levels,
    tr_ref, u_ref, v_ref, kd_ref, lev_ref, forcing_ref, g_ref, rs_ref, rn_ref,
    out_ref, src_ref,
    tr, u, v, kd, vx, ux, lv, mk, q, lap, sm, ratio, red, coup,
    in_sem, out_sem,
):
    lay = Layout(levels)
    rows, cols = lev_ref.shape
    tiles = cols // TILE
    own = slice(PAD, PAD + rows)
    ghost = slice(cols, cols + TILE)

    def inputs(k):
        return (
            pltpu.make_async_copy(tr_ref.at[:, k], tr.at[:, k, own, 0:cols], in_sem.at[0, k]),
            pltpu.make_async_copy(u_ref.at[k], u.at[k], in_sem.at[1, k]),
            pltpu.make_async_copy(v_ref.at[k], v.at[k], in_sem.at[2, k]),
            pltpu.make_async_copy(kd_ref.at[k], kd.at[k], in_sem.at[3, k]),
        )

    def outputs(k):
        return pltpu.make_async_copy(red.at[:, k + 1], out_ref.at[:, k], out_sem.at[k])

    for k in range(levels):
        for copy in inputs(k):
            copy.start()
    for k in range(levels):
        for a in range(2):
            s = 2 * (a * levels + k)
            tr[a, k, PAD - 2 : PAD, 0:cols] = rs_ref[s : s + 2, :]
            tr[a, k, PAD + rows : PAD + rows + 2, 0:cols] = rn_ref[s : s + 2, :]
        s = lay.speed + k
        for t in range(tiles):
            part = slice(t * TILE, (t + 1) * TILE)
            vx[k, t, PAD - 1 : PAD, :] = rs_ref[s : s + 1, part]
            vx[k, t, PAD + rows : PAD + rows + 1, :] = rn_ref[s : s + 1, part]
    for t in range(tiles):
        part = slice(t * TILE, (t + 1) * TILE)
        lv[t, 0:PAD] = jnp.zeros((PAD, TILE), F32)
        lv[t, PAD + rows :] = jnp.zeros((PAD, TILE), F32)
        lv[t, own] = lev_ref[:, part]
        lv[t, PAD - 3 : PAD] = rs_ref[lay.depth : lay.depth + 3, part]
        lv[t, PAD + rows : PAD + rows + 3] = rn_ref[lay.depth : lay.depth + 3, part]
    lv[tiles] = unpacked(g_ref, lay.depth)
    coup[...] = jnp.zeros_like(coup)
    ratio[0] = jnp.zeros_like(ratio[0])
    red[:, 0] = jnp.zeros_like(red[:, 0])
    lane = lane_index((8, TILE))
    lane_last, lane_first = lane == TILE - 1, lane == 0

    def right(parts):
        turned = [pltpu.roll(x, TILE - 1, 1) for x in parts]
        return [jnp.where(lane_last, turned[(t + 1) % (tiles + 1)], turned[t]) for t in range(tiles + 1)]

    def left(parts):
        turned = [pltpu.roll(x, 1, 1) for x in parts]
        return [jnp.where(lane_first, turned[(t + tiles) % (tiles + 1)], turned[t]) for t in range(tiles + 1)]

    for copy in inputs(0):
        copy.wait()

    def down(k, carry):
        later = jnp.minimum(k + 1, levels - 1)

        @pl.when(k + 1 < levels)
        def _():
            for copy in inputs(later):
                copy.wait()

        level = k.astype(F32)
        for t in range(tiles):
            ux[t] = u[k, :, t * TILE : (t + 1) * TILE].astype(F32)
            vx[k, t, own] = v[k, :, t * TILE : (t + 1) * TILE].astype(F32)
        ux[tiles] = unpacked(g_ref, lay.speed + k)[own]
        for a in range(2):
            tr[a, k, :, ghost] = unpacked(g_ref, 2 * (a * levels + k))
        for c in range(0, rows + 2 * PAD, 8):
            here = slice(c, c + 8)
            for t in range(tiles + 1):
                wet = jnp.where(lv[t, here] > level, 1.0, 0.0)
                mk[t, here] = wet
                for a in range(2):
                    q[a, t, here] = wet * tr[a, k, here, t * TILE : (t + 1) * TILE]
        every = range(tiles + 1)
        for c in range(0, rows + 8, 8):
            base = c + PAD - 1
            mid, low, high = slice(base, base + 8), slice(base - 1, base + 7), slice(base + 1, base + 9)
            wet = [mk[t, mid] for t in every]
            e, w = right(wet), left(wet)
            total = [e[t] + w[t] + mk[t, low] + mk[t, high] for t in every]
            for t in every:
                sm[t, c : c + 8] = total[t]
            for a in range(2):
                centre = [q[a, t, mid] for t in every]
                e, w = right(centre), left(centre)
                for t in every:
                    around = e[t] + w[t] + q[a, t, low] + q[a, t, high]
                    lap[a, t, c : c + 8] = wet[t] * (around - centre[t] * total[t])
        for c in range(0, rows, 8):
            base = c + PAD
            mid, low, high = slice(base, base + 8), slice(base - 1, base + 7), slice(base + 1, base + 9)
            here = slice(c, c + 8)
            if c % 16 == 0:
                mixing = kd[later, c : c + 16].astype(F32)
            wet = [mk[t, mid] for t in every]
            speed = [ux[t, here] for t in every]
            wet_e, speed_e = right(wet), right(speed)
            face = [0.25 * (speed[t] + speed_e[t]) * (wet[t] * wet_e[t]) for t in every]
            face_w = left(face)
            wide = [[q[a, t, mid] for t in every] for a in range(2)]
            wide_e, wide_w = [right(x) for x in wide], [left(x) for x in wide]
            bent = [[lap[a, t, c + 1 : c + 9] for t in every] for a in range(2)]
            bent_e, bent_w = [right(x) for x in bent], [left(x) for x in bent]
            for t in range(tiles):
                part = slice(t * TILE, (t + 1) * TILE)
                v_mid = vx[k, t, mid]
                v_north = 0.25 * (v_mid + vx[k, t, high]) * (wet[t] * mk[t, high])
                v_south = 0.25 * (v_mid + vx[k, t, low]) * (wet[t] * mk[t, low])
                spread = face[t] - face_w[t] + v_north - v_south
                total = sm[t, c + 1 : c + 9]
                above = coup[here, part]
                below = jnp.where(lv[t, mid] > level + 1.0, mixing[c % 16 : c % 16 + 8, part], 0.0)
                inverse = 1.0 / (1.0 + above + below + above * ratio[k, here, part])
                ratio[k + 1, here, part] = -below * inverse
                coup[here, part] = below
                for a in range(2):
                    centre = wide[a][t]
                    divergence = (
                        centre * spread
                        + face[t] * wide_e[a][t]
                        - face_w[t] * wide_w[a][t]
                        + v_north * q[a, t, high]
                        - v_south * q[a, t, low]
                    )
                    around = bent_e[a][t] + bent_w[a][t] + lap[a, t, c + 2 : c + 10] + lap[a, t, c : c + 8]
                    lap_two = wet[t] * (around - bent[a][t] * total)
                    value = centre - 0.25 * divergence - 0.01 * lap_two
                    red[a, k + 1, here, part] = (value + above * red[a, k, here, part]) * inverse
        return carry

    lax.fori_loop(0, levels, down, 0)
    outputs(levels - 1).start()
    coup[...] = red[0, levels] - red[1, levels]

    def up(i, carry):
        k = levels - 2 - i
        for c in range(0, rows, 8):
            here = slice(c, c + 8)
            factor = ratio[k + 1, here]
            one = red[0, k + 1, here] - factor * red[0, k + 2, here]
            two = red[1, k + 1, here] - factor * red[1, k + 2, here]
            red[0, k + 1, here] = one
            red[1, k + 1, here] = two
            coup[here] = coup[here] + (one - two)
        outputs(k).start()
        return carry

    lax.fori_loop(0, levels - 1, up, 0)
    src_ref[...] = jnp.where(
        lev_ref[...] > 0.0, forcing_ref[...] + coup[...] * (1.0 / levels), 0.0
    )
    for k in range(levels):
        outputs(k).wait()


def solve_kernel(
    lons, lats, levels,
    src_ref, lev_ref, cw_ref, g_ref, rs_ref, rn_ref,
    out_ref,
    lv, cw, bx, side_in, row_n, row_in, corner_in, part, lon_in, joint, lat_in,
    send_sem, recv_sem, corner_send, corner_recv, lon_send, lon_recv, lat_send, lat_recv,
):
    lay = Layout(levels)
    rows, cols = src_ref.shape
    lon, lat = lax.axis_index("lon"), lax.axis_index("lat")
    east, west = lax.rem(lon + 1, lons), lax.rem(lon + lons - 1, lons)
    mirror = lons - 1 - lon
    top = lat == lats - 1
    bottom = lat == 0
    own = slice(PAD, PAD + rows)
    north_rows = slice(PAD + rows, 2 * PAD + rows)
    ghost = slice(cols, cols + TILE)
    lon_peers = [lax.rem(lon + d, lons) for d in range(1, lons)]
    lat_peers = [lax.rem(lat + d, lats) for d in range(1, lats)]
    barrier = pltpu.get_barrier_semaphore()
    for peer in lon_peers:
        greet(barrier, peer, lat)
    for peer in lat_peers:
        greet(barrier, lon, peer)

    @pl.when(jnp.logical_not(top))
    def _():
        greet(barrier, east, lat + 1)
        greet(barrier, west, lat + 1)

    @pl.when(jnp.logical_not(bottom))
    def _():
        greet(barrier, east, lat - 1)
        greet(barrier, west, lat - 1)

    @pl.when(jnp.logical_not(top))
    def _():
        row_n[...] = src_ref[rows - 8 : rows, :]

    @pl.when(top)
    def _():
        turned = flip_row(src_ref[rows - 8 : rows, :])
        for j in range(8):
            row_n[j : j + 1, :] = turned[7 - j : 8 - j, :]

    @pl.when(bottom)
    def _():
        row_in[0] = jnp.zeros_like(row_in[0])

    peers = lons - 1 + lats - 1

    @pl.when(jnp.logical_or(top, bottom))
    def _():
        pl.semaphore_wait(barrier, peers + 2)

    @pl.when(jnp.logical_not(jnp.logical_or(top, bottom)))
    def _():
        pl.semaphore_wait(barrier, peers + 4)

    to_west = copy_to(src_ref.at[:, 0:TILE], side_in.at[1], send_sem.at[2], recv_sem.at[2], west, lat)
    to_east = copy_to(src_ref.at[:, cols - TILE : cols], side_in.at[0], send_sem.at[3], recv_sem.at[3], east, lat)
    to_west.start()
    to_east.start()
    north_far = copy_to(row_n, row_in.at[1], send_sem.at[0], recv_sem.at[0], mirror, lat)
    north_near = copy_to(row_n, row_in.at[0], send_sem.at[0], recv_sem.at[1], lon, lat + 1)
    south = copy_to(src_ref.at[0:8, :], row_in.at[1], send_sem.at[1], recv_sem.at[0], lon, lat - 1)
    pl.when(top)(north_far.start)
    pl.when(jnp.logical_not(top))(north_near.start)
    pl.when(jnp.logical_not(bottom))(south.start)

    corners = Corners(
        lons, lats,
        (
            src_ref.at[rows - 8 : rows, 0:TILE], src_ref.at[rows - 8 : rows, cols - TILE : cols],
            src_ref.at[0:8, 0:TILE], src_ref.at[0:8, cols - TILE : cols],
        ),
        (row_n.at[:, cols - TILE : cols], row_n.at[:, 0:TILE]),
        corner_in, corner_send, corner_recv,
    )
    corners.start()
    for plane, own_ref, slot, empty in ((lv, lev_ref, lay.depth, 0.0), (cw, cw_ref, lay.weight, 1.0)):
        plane[...] = jnp.full(plane.shape, empty, F32)
        plane[own, 0:cols] = own_ref[...]
        plane[PAD - 3 : PAD, 0:cols] = rs_ref[slot : slot + 3, :]
        plane[PAD + rows : PAD + rows + 3, 0:cols] = rn_ref[slot : slot + 3, :]
        plane[:, ghost] = unpacked(g_ref, slot)
    wet = lv[...] > 0.0
    cw[...] = jnp.where(wet, cw[...], 1.0)
    lv[...] = jnp.where(wet, 1.0 / cw[...], 0.0)
    bx[own, 0:cols] = src_ref[...]

    to_west.wait_recv()
    to_east.wait_recv()
    lane = lane_index((rows, TILE))
    bx[own, ghost] = jnp.where(lane < TILE // 2, side_in[1], side_in[0])
    north_far.wait_recv()
    bx[north_rows, 0:cols] = row_in[1]
    pl.when(jnp.logical_not(bottom))(north_near.wait_recv)
    bx[0:PAD, 0:cols] = row_in[0]
    corners.wait_recv()
    lane = lane_index((8, TILE))
    bx[north_rows, ghost] = jnp.where(lane < TILE // 2, corner_in[1, 1], corner_in[1, 0])
    bx[0:PAD, ghost] = jnp.where(lane < TILE // 2, corner_in[0, 1], corner_in[0, 0])

    height, width = bx.shape

    def operator(field):
        sides = pltpu.roll(field, 1, 1) + pltpu.roll(field, width - 1, 1)
        triple = field + 0.5 * sides
        ends = pltpu.roll(triple, 1, 0) + pltpu.roll(triple, height - 1, 0)
        return cw[...] * field - sides - ends

    zero = lv[...] * bx[...]
    image_zero = operator(zero)
    one = lv[...] * image_zero - zero
    image_one = operator(one)
    two = 2.0 * (lv[...] * image_one - one) - zero
    image_two = operator(two)

    def inner(value):
        return value[own, 0:cols]

    base = [inner(zero), inner(one), inner(two)]
    images = [inner(image_zero), inner(image_one), inner(image_two)]
    source = src_ref[...]
    pairs = [
        (base[0], images[0]), (base[1], images[0]), (base[2], images[0]),
        (base[1], images[1]), (base[2], images[1]), (base[2], images[2]),
        (base[0], source), (base[1], source), (base[2], source),
    ]
    part[8:16, :] = jnp.zeros((8, TILE), F32)
    for i, (x, y) in enumerate(pairs):
        line = jnp.sum(x * y, axis=0, keepdims=True)
        part[i : i + 1, :] = sum(line[:, t : t + TILE] for t in range(0, cols, TILE))
    over_lon = [
        copy_to(part, lon_in.at[d], lon_send.at[d], lon_recv.at[d], peer, lat)
        for d, peer in enumerate(lon_peers)
    ]
    for copy in over_lon:
        copy.start()
    for copy in over_lon:
        copy.wait_recv()
    joint[...] = part[...] + jnp.sum(lon_in[...], axis=0)
    over_lat = [
        copy_to(joint, lat_in.at[d], lat_send.at[d], lat_recv.at[d], lon, peer)
        for d, peer in enumerate(lat_peers)
    ]
    for copy in over_lat:
        copy.start()
    for copy in over_lat:
        copy.wait_recv()
    totals = jnp.sum(joint[...] + jnp.sum(lat_in[...], axis=0), axis=1, keepdims=True)
    g00, g01, g02, g11, g12, g22, d0, d1, d2 = (totals[i : i + 1, :] for i in range(9))
    small = 1e-9 * g00
    l10, l20 = g01 / g00, g02 / g00
    pivot_one = g11 - l10 * g01
    inverse_one = jnp.where(pivot_one > small, 1.0 / pivot_one, 0.0)
    cross = g12 - l20 * g01
    l21 = cross * inverse_one
    pivot_two = g22 - l20 * g02 - l21 * cross
    inverse_two = jnp.where(pivot_two > small, 1.0 / pivot_two, 0.0)
    y1 = d1 - l10 * d0
    y2 = d2 - l20 * d0 - l21 * y1
    c2 = y2 * inverse_two
    c1 = y1 * inverse_one - l21 * c2
    c0 = d0 / g00 - l10 * c1 - l20 * c2
    out_ref[...] = c0 * base[0] + c1 * base[1] + c2 * base[2]

    to_west.wait_send()
    to_east.wait_send()
    north_far.wait_send()
    pl.when(jnp.logical_not(bottom))(south.wait_send)
    corners.wait_send()
    for copy in over_lon + over_lat:
        copy.wait_send()


def shards(
    lons, lats,
    tracers, east_velocity, north_velocity, vertical_diffusivity,
    depth_levels, ocean_blocks, forcing, surface_coupling,
):
    levels, rows, cols = tracers.shape[1:]
    lay = Layout(levels)
    high, wide, tiles = rows + 2 * PAD, cols + TILE, cols // TILE
    dma = pltpu.SemaphoreType.DMA
    strip = jax.ShapeDtypeStruct((lay.rows, cols), F32)
    bf16 = jnp.bfloat16
    plane = jax.ShapeDtypeStruct((rows, cols), F32)
    ghosts, south, north, depth, weight = pl.pallas_call(
        functools.partial(ghost_kernel, lons, lats, levels),
        out_shape=(jax.ShapeDtypeStruct((2, high, TILE), F32), strip, strip, plane, plane),
        in_specs=[HBM, HBM, HBM, VMEM, pl.BlockSpec(memory_space=pltpu.SMEM), VMEM],
        out_specs=(VMEM,) * 5,
        scratch_shapes=[
            pltpu.VMEM((2, levels, rows, TILE), F32),
            pltpu.VMEM((2, levels, rows, TILE), F32),
            pltpu.VMEM((2, levels, 8, cols), F32),
            pltpu.VMEM((2, levels, 8, cols), F32),
            pltpu.VMEM((levels, rows, TILE), bf16),
            pltpu.VMEM((levels, rows, TILE), bf16),
            pltpu.VMEM((levels, 16, cols), bf16),
            pltpu.VMEM((levels, 16, cols), bf16),
            pltpu.VMEM((rows, TILE), F32),
            pltpu.VMEM((rows, TILE), F32),
            pltpu.VMEM((lay.rows, cols), F32),
            pltpu.VMEM((lay.rows, cols), F32),
            pltpu.VMEM((2, PAD, TILE), F32),
            pltpu.VMEM((2, 2, PAD, TILE), F32),
            pltpu.VMEM((2, rows, TILE), F32),
            pltpu.VMEM((lay.rows, cols), F32),
            pltpu.VMEM((lay.rows, cols), F32),
            dma((8,)), dma((4,)), dma((4,)), dma((4,)), dma((4,)),
        ],
        compiler_params=pltpu.CompilerParams(
            collective_id=0, has_side_effects=True, vmem_limit_bytes=32 << 20
        ),
        name="ghosts",
    )(tracers, east_velocity, north_velocity, depth_levels, ocean_blocks, surface_coupling)
    new_tracers, source = pl.pallas_call(
        functools.partial(column_kernel, levels),
        out_shape=(
            jax.ShapeDtypeStruct(tracers.shape, F32),
            jax.ShapeDtypeStruct((rows, cols), F32),
        ),
        in_specs=[HBM] * 4 + [VMEM] * 5,
        out_specs=(HBM, VMEM),
        scratch_shapes=[
            pltpu.VMEM((2, levels, high, wide), F32),
            pltpu.VMEM((levels, rows, cols), bf16),
            pltpu.VMEM((levels, rows, cols), bf16),
            pltpu.VMEM((levels, rows, cols), bf16),
            pltpu.VMEM((levels, tiles, high, TILE), F32),
            pltpu.VMEM((tiles + 1, rows, TILE), F32),
            pltpu.VMEM((tiles + 1, high, TILE), F32),
            pltpu.VMEM((tiles + 1, high, TILE), F32),
            pltpu.VMEM((2, tiles + 1, high, TILE), F32),
            pltpu.VMEM((2, tiles + 1, high, TILE), F32),
            pltpu.VMEM((tiles + 1, high, TILE), F32),
            pltpu.VMEM((levels + 1, rows, cols), F32),
            pltpu.VMEM((2, levels + 1, rows, cols), F32),
            pltpu.VMEM((rows, cols), F32),
            dma((4, levels)), dma((levels,)),
        ],
        compiler_params=pltpu.CompilerParams(vmem_limit_bytes=48 << 20),
        name="columns",
    )(tracers, east_velocity, north_velocity, vertical_diffusivity, depth, forcing, ghosts, south, north)
    surface = pl.pallas_call(
        functools.partial(solve_kernel, lons, lats, levels),
        out_shape=jax.ShapeDtypeStruct((rows, cols), F32),
        in_specs=[VMEM] * 6,
        out_specs=VMEM,
        scratch_shapes=[
            pltpu.VMEM((high, wide), F32),
            pltpu.VMEM((high, wide), F32),
            pltpu.VMEM((high, wide), F32),
            pltpu.VMEM((2, rows, TILE), F32),
            pltpu.VMEM((8, cols), F32),
            pltpu.VMEM((2, 8, cols), F32),
            pltpu.VMEM((2, 2, 8, TILE), F32),
            pltpu.VMEM((16, TILE), F32),
            pltpu.VMEM((lons - 1, 16, TILE), F32),
            pltpu.VMEM((16, TILE), F32),
            pltpu.VMEM((lats - 1, 16, TILE), F32),
            dma((4,)), dma((4,)), dma((4,)), dma((4,)),
            dma((lons - 1,)), dma((lons - 1,)), dma((lats - 1,)), dma((lats - 1,)),
        ],
        compiler_params=pltpu.CompilerParams(
            collective_id=1, has_side_effects=True, vmem_limit_bytes=32 << 20
        ),
        name="surface",
    )(source, depth, weight, ghosts, south, north)
    return new_tracers, surface


def solution(mesh):
    flat = P("lat", "lon")
    deep = P(None, "lat", "lon")
    tracer = P(None, None, "lat", "lon")
    return jax.shard_map(
        functools.partial(shards, mesh.shape["lon"], mesh.shape["lat"]),
        mesh=mesh,
        in_specs=(tracer, deep, deep, deep, flat, flat, flat, flat),
        out_specs=(tracer, flat),
        check_vma=False,
    )
```

```python
import functools

import jax
import jax.numpy as jnp
from jax import lax
from jax.experimental import pallas as pl
from jax.experimental.pallas import tpu as pltpu
from jax.sharding import PartitionSpec as P

F32 = jnp.float32
MESH = pl.DeviceIdType.MESH
VMEM = pl.BlockSpec(memory_space=pltpu.VMEM)
HBM = pl.BlockSpec(memory_space=pltpu.HBM)
PAD = 8
TILE = 128


def lane_index(shape):
    return lax.broadcasted_iota(jnp.int32, shape, len(shape) - 1)


def flip_tile(value):
    lane = lane_index(value.shape)
    for bit in range(7):
        step = 1 << bit
        value = jnp.where(
            lane & step != 0, pltpu.roll(value, step, 1), pltpu.roll(value, TILE - step, 1)
        )
    return value


def flip_row(value):
    tiles = value.shape[1] // TILE
    return jnp.concatenate(
        [flip_tile(value[:, t * TILE : (t + 1) * TILE]) for t in reversed(range(tiles))], axis=1
    )


def shift_lanes(value, by):
    width = value.shape[1]
    by = by % width
    return value if by == 0 else pltpu.roll(value, by, 1)


class Layout:
    def __init__(self, levels):
        self.levels = levels
        self.speed = 4 * levels
        self.depth = 5 * levels
        self.weight = 5 * levels + 3
        self.count = 5 * levels + 6
        self.rows = -(-self.count // 8) * 8


def copy_to(src, dst, send, recv, lon, lat):
    return pltpu.make_async_remote_copy(
        src_ref=src,
        dst_ref=dst,
        send_sem=send,
        recv_sem=recv,
        device_id={"lon": lon, "lat": lat},
        device_id_type=MESH,
    )


def greet(barrier, lon, lat):
    pl.semaphore_signal(barrier, inc=1, device_id={"lon": lon, "lat": lat}, device_id_type=MESH)


class Corners:
    def __init__(self, lons, lats, sources, turned, dst, send, recv):
        lon, lat = lax.axis_index("lon"), lax.axis_index("lat")
        east, west = lax.rem(lon + 1, lons), lax.rem(lon + lons - 1, lons)
        self.top, self.bottom = lat == lats - 1, lat == 0
        far_first, far_last = lax.rem(lons - lon, lons), lax.rem(2 * lons - 2 - lon, lons)
        self.own_first = jnp.logical_and(self.top, far_first == lon)
        self.own_last = jnp.logical_and(self.top, far_last == lon)
        self.turned, self.dst = turned, dst
        high_first, high_last, low_first, low_last = sources
        turned_first, turned_last = turned
        self.up_last = copy_to(high_last, dst.at[0, 0], send.at[0], recv.at[0], east, lat + 1)
        self.up_first = copy_to(high_first, dst.at[0, 1], send.at[1], recv.at[1], west, lat + 1)
        self.far_first = copy_to(turned_first, dst.at[1, 0], send.at[1], recv.at[2], far_first, lat)
        self.far_last = copy_to(turned_last, dst.at[1, 1], send.at[0], recv.at[3], far_last, lat)
        self.down_last = copy_to(low_last, dst.at[1, 0], send.at[2], recv.at[2], east, lat - 1)
        self.down_first = copy_to(low_first, dst.at[1, 1], send.at[3], recv.at[3], west, lat - 1)

    def start(self):
        @pl.when(jnp.logical_not(self.top))
        def _():
            self.up_last.start()
            self.up_first.start()

        @pl.when(jnp.logical_not(self.bottom))
        def _():
            self.down_last.start()
            self.down_first.start()

        pl.when(jnp.logical_and(self.top, jnp.logical_not(self.own_first)))(self.far_first.start)
        pl.when(jnp.logical_and(self.top, jnp.logical_not(self.own_last)))(self.far_last.start)

        @pl.when(self.own_first)
        def _():
            self.dst[1, 0] = self.turned[0][...]

        @pl.when(self.own_last)
        def _():
            self.dst[1, 1] = self.turned[1][...]

        @pl.when(self.bottom)
        def _():
            self.dst[0] = jnp.zeros_like(self.dst[0])

    def wait_recv(self):
        @pl.when(jnp.logical_not(self.bottom))
        def _():
            self.up_last.wait_recv()
            self.up_first.wait_recv()

        pl.when(jnp.logical_not(self.own_first))(self.far_first.wait_recv)
        pl.when(jnp.logical_not(self.own_last))(self.far_last.wait_recv)

    def wait_send(self):
        pl.when(jnp.logical_not(self.own_last))(self.up_last.wait_send)
        pl.when(jnp.logical_not(self.own_first))(self.up_first.wait_send)

        @pl.when(jnp.logical_not(self.bottom))
        def _():
            self.down_last.wait_send()
            self.down_first.wait_send()


def ghost_kernel(
    lons, lats, levels,
    tr_ref, u_ref, v_ref, depth_hbm, ocean_ref, coupling_hbm,
    g_out, rs_out, rn_out, lev_ref, cw_ref,
    depth_ref, coupling_ref, t_w, t_e, t_s, t_n, u_w, u_e, v_s, v_n,
    p_w, p_e, r_s, r_n, turned, corner_in, g_in, rs_in, rn_in,
    local_sem, send_sem, recv_sem, corner_send, corner_recv,
):
    lay = Layout(levels)
    lon, lat = lax.axis_index("lon"), lax.axis_index("lat")
    rows, cols = depth_ref.shape
    east, west = lax.rem(lon + 1, lons), lax.rem(lon + lons - 1, lons)
    mirror = lons - 1 - lon
    top = lat == lats - 1
    bottom = lat == 0
    locals_ = [
        pltpu.make_async_copy(src, dst, local_sem.at[i])
        for i, (src, dst) in enumerate(
            (
                (depth_hbm, depth_ref),
                (coupling_hbm, coupling_ref),
                (tr_ref.at[:, :, 0:8, :], t_s),
                (tr_ref.at[:, :, rows - 8 : rows, :], t_n),
                (v_ref.at[:, 0:16, :], v_s),
                (v_ref.at[:, rows - 16 : rows, :], v_n),
                (tr_ref.at[:, :, :, 0:TILE], t_w),
                (tr_ref.at[:, :, :, cols - TILE : cols], t_e),
                (u_ref.at[:, :, 0:TILE], u_w),
                (u_ref.at[:, :, cols - TILE : cols], u_e),
            )
        )
    ]
    for copy in locals_:
        copy.start()
    barrier = pltpu.get_barrier_semaphore()
    greet(barrier, east, lat)
    greet(barrier, west, lat)

    @pl.when(top)
    def _():
        greet(barrier, mirror, lat)

        greet(barrier, lax.rem(lons - lon, lons), lat)
        greet(barrier, lax.rem(2 * lons - 2 - lon, lons), lat)

    @pl.when(jnp.logical_not(top))
    def _():
        for peer in (lon, east, west):
            greet(barrier, peer, lat + 1)

    @pl.when(jnp.logical_not(bottom))
    def _():
        for peer in (lon, east, west):
            greet(barrier, peer, lat - 1)

    @pl.when(bottom)
    def _():
        rs_in[...] = jnp.zeros_like(rs_in)

    for copy in locals_[0:2]:
        copy.wait()
    row = lax.broadcasted_iota(jnp.int32, (rows, cols), 0)
    col = lane_index((rows, cols))
    tall, broad = rows // ocean_ref.shape[0], cols // ocean_ref.shape[1]
    cells = jnp.zeros((rows, cols), jnp.int32)
    for i in range(ocean_ref.shape[0]):
        for j in range(ocean_ref.shape[1]):
            inside = (row >= i * tall) & (row < (i + 1) * tall) & (col >= j * broad) & (col < (j + 1) * broad)
            cells = jnp.where(inside, ocean_ref[i, j], cells)
    lev_ref[...] = jnp.where(cells > 0, depth_ref[...], 0).astype(F32)
    cw_ref[...] = 6.0 + coupling_ref[...]
    for copy in locals_[2:6]:
        copy.wait()
    tail = 8 * (lay.depth // 8)
    r_s[tail:, :] = jnp.zeros_like(r_s[tail:, :])
    r_n[tail:, :] = jnp.zeros_like(r_n[tail:, :])
    for a in range(2):
        for k in range(levels):
            s = 2 * (a * levels + k)
            r_s[s : s + 2, :] = t_s[a, k, 0:2, :]
    for k in range(levels):
        r_s[lay.speed + k : lay.speed + k + 1, :] = v_s[k].astype(F32)[0:1, :]
    r_s[lay.depth : lay.depth + 3, :] = lev_ref[0:3, :]
    r_s[lay.weight : lay.weight + 3, :] = cw_ref[0:3, :]

    @pl.when(jnp.logical_not(top))
    def _():
        for a in range(2):
            for k in range(levels):
                s = 2 * (a * levels + k)
                r_n[s : s + 2, :] = t_n[a, k, 6:8, :]
        for k in range(levels):
            r_n[lay.speed + k : lay.speed + k + 1, :] = v_n[k].astype(F32)[15:16, :]
        r_n[lay.depth : lay.depth + 3, :] = lev_ref[rows - 3 : rows, :]
        r_n[lay.weight : lay.weight + 3, :] = cw_ref[rows - 3 : rows, :]

    @pl.when(top)
    def _():
        for a in range(2):
            for k in range(levels):
                s = 2 * (a * levels + k)
                r_n[s : s + 1, :] = t_n[a, k, 7:8, :]
                r_n[s + 1 : s + 2, :] = t_n[a, k, 6:7, :]
        for k in range(levels):
            r_n[lay.speed + k : lay.speed + k + 1, :] = -v_n[k].astype(F32)[15:16, :]
        for j in range(3):
            r_n[lay.depth + j : lay.depth + j + 1, :] = lev_ref[rows - 1 - j : rows - j, :]
            r_n[lay.weight + j : lay.weight + j + 1, :] = cw_ref[rows - 1 - j : rows - j, :]
        r_n[...] = flip_row(r_n[...])

    @pl.when(bottom)
    def _():
        pl.semaphore_wait(barrier, 5)

    @pl.when(top)
    def _():
        pl.semaphore_wait(barrier, 8)

    @pl.when(jnp.logical_not(jnp.logical_or(top, bottom)))
    def _():
        pl.semaphore_wait(barrier, 8)

    north_far = copy_to(r_n, rn_in, send_sem.at[0], recv_sem.at[0], mirror, lat)
    north_near = copy_to(r_n, rs_in, send_sem.at[0], recv_sem.at[1], lon, lat + 1)
    south = copy_to(r_s, rn_in, send_sem.at[1], recv_sem.at[0], lon, lat - 1)
    pl.when(top)(north_far.start)
    pl.when(jnp.logical_not(top))(north_near.start)
    pl.when(jnp.logical_not(bottom))(south.start)

    for copy in locals_[6:]:
        copy.wait()
    lane = lane_index((rows, TILE))
    back = TILE - 1 - lane
    first, last = jnp.zeros((rows, TILE), F32), jnp.zeros((rows, TILE), F32)
    for a in range(2):
        for k in range(levels):
            s = 2 * (a * levels + k)
            first = jnp.where(lane >> 1 == s // 2, shift_lanes(t_w[a, k], s), first)
            last = jnp.where(back >> 1 == s // 2, shift_lanes(t_e[a, k], -s), last)
    for k in range(levels):
        s = lay.speed + k
        first = jnp.where(lane == s, shift_lanes(u_w[k].astype(F32), s), first)
        last = jnp.where(back == s, shift_lanes(u_e[k].astype(F32), -s), last)
    for ref, s in ((lev_ref, lay.depth), (cw_ref, lay.weight)):
        inside = jnp.logical_and(lane >= s, lane < s + 3)
        first = jnp.where(inside, shift_lanes(ref[:, 0:TILE], s), first)
        inside = jnp.logical_and(back >= s, back < s + 3)
        last = jnp.where(inside, shift_lanes(ref[:, cols - TILE : cols], -s), last)
    p_w[...] = first
    p_e[...] = last
    own = slice(PAD, PAD + rows)
    to_west = copy_to(p_w, g_in.at[1], send_sem.at[2], recv_sem.at[2], west, lat)
    to_east = copy_to(p_e, g_in.at[0], send_sem.at[3], recv_sem.at[3], east, lat)
    to_west.start()
    to_east.start()

    @pl.when(top)
    def _():
        for side, value in enumerate((first, last)):
            back_tile = flip_tile(value[rows - PAD : rows, :])
            for j in range(PAD):
                turned[side, j : j + 1, :] = back_tile[PAD - 1 - j : PAD - j, :]

    corners = Corners(
        lons, lats,
        (p_w.at[rows - PAD : rows, :], p_e.at[rows - PAD : rows, :], p_w.at[0:PAD, :], p_e.at[0:PAD, :]),
        (turned.at[0], turned.at[1]),
        corner_in, corner_send, corner_recv,
    )
    corners.start()
    north_far.wait_recv()
    rn_out[...] = rn_in[...]
    pl.when(jnp.logical_not(bottom))(north_near.wait_recv)
    rs_out[...] = rs_in[...]
    to_west.wait_recv()
    to_east.wait_recv()
    g_out[:, own, :] = g_in[...]
    corners.wait_recv()
    g_out[:, 0:PAD, :] = corner_in[0]
    g_out[:, PAD + rows : 2 * PAD + rows, :] = corner_in[1]
    north_far.wait_send()
    to_west.wait_send()
    to_east.wait_send()
    pl.when(jnp.logical_not(bottom))(south.wait_send)
    corners.wait_send()


def unpacked(g_ref, slot):
    lane = lane_index(g_ref.shape[1:])
    return jnp.where(
        lane < TILE // 2,
        pltpu.roll(g_ref[1], TILE - slot, 1),
        pltpu.roll(g_ref[0], slot, 1),
    )


def column_kernel(
    levels,
    tr_ref, u_ref, v_ref, kd_ref, forcing_hbm, lev_ref, g_ref, rs_ref, rn_ref,
    out_ref, src_ref,
    forcing_ref, tr, u, v, kd, vx, ux, lv, mk, q, lap, sm, ratio, red, coup,
    in_sem, out_sem, forcing_sem,
):
    lay = Layout(levels)
    rows, cols = lev_ref.shape
    tiles = cols // TILE
    own = slice(PAD, PAD + rows)
    ghost = slice(cols, cols + TILE)

    def inputs(k):
        return (
            pltpu.make_async_copy(tr_ref.at[:, k], tr.at[:, k, own, 0:cols], in_sem.at[0, k]),
            pltpu.make_async_copy(u_ref.at[k], u.at[k], in_sem.at[1, k]),
            pltpu.make_async_copy(v_ref.at[k], v.at[k], in_sem.at[2, k]),
            pltpu.make_async_copy(kd_ref.at[k], kd.at[k], in_sem.at[3, k]),
        )

    def outputs(k):
        return pltpu.make_async_copy(red.at[:, k + 1], out_ref.at[:, k], out_sem.at[k])

    for k in range(levels):
        for copy in inputs(k):
            copy.start()
    forcing_copy = pltpu.make_async_copy(forcing_hbm, forcing_ref, forcing_sem)
    forcing_copy.start()
    for k in range(levels):
        for a in range(2):
            s = 2 * (a * levels + k)
            tr[a, k, PAD - 2 : PAD, 0:cols] = rs_ref[s : s + 2, :]
            tr[a, k, PAD + rows : PAD + rows + 2, 0:cols] = rn_ref[s : s + 2, :]
        s = lay.speed + k
        for t in range(tiles):
            part = slice(t * TILE, (t + 1) * TILE)
            vx[k, t, PAD - 1 : PAD, :] = rs_ref[s : s + 1, part]
            vx[k, t, PAD + rows : PAD + rows + 1, :] = rn_ref[s : s + 1, part]
    for t in range(tiles):
        part = slice(t * TILE, (t + 1) * TILE)
        lv[t, 0:PAD] = jnp.zeros((PAD, TILE), F32)
        lv[t, PAD + rows :] = jnp.zeros((PAD, TILE), F32)
        lv[t, own] = lev_ref[:, part]
        lv[t, PAD - 3 : PAD] = rs_ref[lay.depth : lay.depth + 3, part]
        lv[t, PAD + rows : PAD + rows + 3] = rn_ref[lay.depth : lay.depth + 3, part]
    lv[tiles] = unpacked(g_ref, lay.depth)
    coup[...] = jnp.zeros_like(coup)
    ratio[0] = jnp.zeros_like(ratio[0])
    red[:, 0] = jnp.zeros_like(red[:, 0])
    lane = lane_index((8, TILE))
    lane_last, lane_first = lane == TILE - 1, lane == 0

    def right(parts):
        turned = [pltpu.roll(x, TILE - 1, 1) for x in parts]
        return [jnp.where(lane_last, turned[(t + 1) % (tiles + 1)], turned[t]) for t in range(tiles + 1)]

    def left(parts):
        turned = [pltpu.roll(x, 1, 1) for x in parts]
        return [jnp.where(lane_first, turned[(t + tiles) % (tiles + 1)], turned[t]) for t in range(tiles + 1)]

    for copy in inputs(0):
        copy.wait()

    def down(k, carry):
        later = jnp.minimum(k + 1, levels - 1)

        @pl.when(k + 1 < levels)
        def _():
            for copy in inputs(later):
                copy.wait()

        level = k.astype(F32)
        for t in range(tiles):
            ux[t] = u[k, :, t * TILE : (t + 1) * TILE].astype(F32)
            vx[k, t, own] = v[k, :, t * TILE : (t + 1) * TILE].astype(F32)
        ux[tiles] = unpacked(g_ref, lay.speed + k)[own]
        for a in range(2):
            tr[a, k, :, ghost] = unpacked(g_ref, 2 * (a * levels + k))
        for c in range(0, rows + 2 * PAD, 8):
            here = slice(c, c + 8)
            for t in range(tiles + 1):
                wet = jnp.where(lv[t, here] > level, 1.0, 0.0)
                mk[t, here] = wet
                for a in range(2):
                    q[a, t, here] = wet * tr[a, k, here, t * TILE : (t + 1) * TILE]
        every = range(tiles + 1)
        for c in range(0, rows + 8, 8):
            base = c + PAD - 1
            mid, low, high = slice(base, base + 8), slice(base - 1, base + 7), slice(base + 1, base + 9)
            wet = [mk[t, mid] for t in every]
            e, w = right(wet), left(wet)
            total = [e[t] + w[t] + mk[t, low] + mk[t, high] for t in every]
            rate = [0.01 * x for x in wet]
            for t in every:
                sm[t, c : c + 8] = total[t]
            for a in range(2):
                centre = [q[a, t, mid] for t in every]
                e, w = right(centre), left(centre)
                for t in every:
                    around = e[t] + w[t] + q[a, t, low] + q[a, t, high]
                    lap[a, t, c : c + 8] = rate[t] * (around - centre[t] * total[t])
        for c in range(0, rows, 8):
            base = c + PAD
            mid, low, high = slice(base, base + 8), slice(base - 1, base + 7), slice(base + 1, base + 9)
            here = slice(c, c + 8)
            if c % 16 == 0:
                mixing = kd[later, c : c + 16].astype(F32)
            wet = [mk[t, mid] for t in every]
            speed = [ux[t, here] for t in every]
            wet_e, speed_e = right(wet), right(speed)
            face = [0.0625 * (speed[t] + speed_e[t]) * (wet[t] * wet_e[t]) for t in every]
            face_w = left(face)
            shared = []
            for t in range(tiles):
                part = slice(t * TILE, (t + 1) * TILE)
                v_mid = vx[k, t, mid]
                scaled = 0.0625 * wet[t]
                v_north = (v_mid + vx[k, t, high]) * (scaled * mk[t, high])
                v_south = (v_mid + vx[k, t, low]) * (scaled * mk[t, low])
                keep = 1.0 - (face[t] - face_w[t] + v_north - v_south)
                above = coup[here, part]
                below = jnp.where(lv[t, mid] > level + 1.0, mixing[c % 16 : c % 16 + 8, part], 0.0)
                inverse = 1.0 / (1.0 + above + below + above * ratio[k, here, part])
                ratio[k + 1, here, part] = -below * inverse
                coup[here, part] = below
                shared.append((v_north, v_south, keep, above, inverse))
            for a in range(2):
                wide = [q[a, t, mid] for t in every]
                wide_e, wide_w = right(wide), left(wide)
                partial = []
                for t in range(tiles):
                    v_north, v_south, keep, above, inverse = shared[t]
                    part = slice(t * TILE, (t + 1) * TILE)
                    partial.append(
                        wide[t] * keep
                        - face[t] * wide_e[t]
                        + face_w[t] * wide_w[t]
                        - v_north * q[a, t, high]
                        + v_south * q[a, t, low]
                    )
                bent = [lap[a, t, c + 1 : c + 9] for t in every]
                bent_e, bent_w = right(bent), left(bent)
                for t in range(tiles):
                    v_north, v_south, keep, above, inverse = shared[t]
                    part = slice(t * TILE, (t + 1) * TILE)
                    around = bent_e[t] + bent_w[t] + lap[a, t, c + 2 : c + 10] + lap[a, t, c : c + 8]
                    value = partial[t] - wet[t] * (around - bent[t] * sm[t, c + 1 : c + 9])
                    red[a, k + 1, here, part] = (value + above * red[a, k, here, part]) * inverse
        return carry

    lax.fori_loop(0, levels, down, 0)
    outputs(levels - 1).start()
    coup[...] = red[0, levels] - red[1, levels]

    def up(i, carry):
        k = levels - 2 - i
        for c in range(0, rows, 8):
            here = slice(c, c + 8)
            factor = ratio[k + 1, here]
            one = red[0, k + 1, here] - factor * red[0, k + 2, here]
            two = red[1, k + 1, here] - factor * red[1, k + 2, here]
            red[0, k + 1, here] = one
            red[1, k + 1, here] = two
            coup[here] = coup[here] + (one - two)
        outputs(k).start()
        return carry

    lax.fori_loop(0, levels - 1, up, 0)
    forcing_copy.wait()
    src_ref[...] = jnp.where(
        lev_ref[...] > 0.0, forcing_ref[...] + coup[...] * (1.0 / levels), 0.0
    )
    for k in range(levels):
        outputs(k).wait()


def solve_kernel(
    lons, lats, levels,
    src_ref, lev_ref, cw_ref, g_ref, rs_ref, rn_ref,
    out_ref,
    lv, cw, bx, side_in, row_n, row_in, corner_in, part, lon_in, joint, lat_in,
    send_sem, recv_sem, corner_send, corner_recv, lon_send, lon_recv, lat_send, lat_recv,
):
    lay = Layout(levels)
    rows, cols = src_ref.shape
    lon, lat = lax.axis_index("lon"), lax.axis_index("lat")
    east, west = lax.rem(lon + 1, lons), lax.rem(lon + lons - 1, lons)
    mirror = lons - 1 - lon
    top = lat == lats - 1
    bottom = lat == 0
    own = slice(PAD, PAD + rows)
    north_rows = slice(PAD + rows, 2 * PAD + rows)
    ghost = slice(cols, cols + TILE)
    lon_peers = [lax.rem(lon + d, lons) for d in range(1, lons)]
    lat_peers = [lax.rem(lat + d, lats) for d in range(1, lats)]
    barrier = pltpu.get_barrier_semaphore()
    for peer in lon_peers:
        greet(barrier, peer, lat)
    for peer in lat_peers:
        greet(barrier, lon, peer)

    @pl.when(jnp.logical_not(top))
    def _():
        greet(barrier, east, lat + 1)
        greet(barrier, west, lat + 1)

    @pl.when(jnp.logical_not(bottom))
    def _():
        greet(barrier, east, lat - 1)
        greet(barrier, west, lat - 1)

    @pl.when(jnp.logical_not(top))
    def _():
        row_n[...] = src_ref[rows - 8 : rows, :]

    @pl.when(top)
    def _():
        turned = flip_row(src_ref[rows - 8 : rows, :])
        for j in range(8):
            row_n[j : j + 1, :] = turned[7 - j : 8 - j, :]

    @pl.when(bottom)
    def _():
        row_in[0] = jnp.zeros_like(row_in[0])

    peers = lons - 1 + lats - 1

    @pl.when(jnp.logical_or(top, bottom))
    def _():
        pl.semaphore_wait(barrier, peers + 2)

    @pl.when(jnp.logical_not(jnp.logical_or(top, bottom)))
    def _():
        pl.semaphore_wait(barrier, peers + 4)

    to_west = copy_to(src_ref.at[:, 0:TILE], side_in.at[1], send_sem.at[2], recv_sem.at[2], west, lat)
    to_east = copy_to(src_ref.at[:, cols - TILE : cols], side_in.at[0], send_sem.at[3], recv_sem.at[3], east, lat)
    to_west.start()
    to_east.start()
    north_far = copy_to(row_n, row_in.at[1], send_sem.at[0], recv_sem.at[0], mirror, lat)
    north_near = copy_to(row_n, row_in.at[0], send_sem.at[0], recv_sem.at[1], lon, lat + 1)
    south = copy_to(src_ref.at[0:8, :], row_in.at[1], send_sem.at[1], recv_sem.at[0], lon, lat - 1)
    pl.when(top)(north_far.start)
    pl.when(jnp.logical_not(top))(north_near.start)
    pl.when(jnp.logical_not(bottom))(south.start)

    corners = Corners(
        lons, lats,
        (
            src_ref.at[rows - 8 : rows, 0:TILE], src_ref.at[rows - 8 : rows, cols - TILE : cols],
            src_ref.at[0:8, 0:TILE], src_ref.at[0:8, cols - TILE : cols],
        ),
        (row_n.at[:, cols - TILE : cols], row_n.at[:, 0:TILE]),
        corner_in, corner_send, corner_recv,
    )
    corners.start()
    for plane, own_ref, slot, empty in ((lv, lev_ref, lay.depth, 0.0), (cw, cw_ref, lay.weight, 1.0)):
        plane[...] = jnp.full(plane.shape, empty, F32)
        plane[own, 0:cols] = own_ref[...]
        plane[PAD - 3 : PAD, 0:cols] = rs_ref[slot : slot + 3, :]
        plane[PAD + rows : PAD + rows + 3, 0:cols] = rn_ref[slot : slot + 3, :]
        plane[:, ghost] = unpacked(g_ref, slot)
    wet = lv[...] > 0.0
    cw[...] = jnp.where(wet, cw[...], 1.0)
    lv[...] = jnp.where(wet, 1.0 / cw[...], 0.0)
    bx[own, 0:cols] = src_ref[...]

    to_west.wait_recv()
    to_east.wait_recv()
    lane = lane_index((rows, TILE))
    bx[own, ghost] = jnp.where(lane < TILE // 2, side_in[1], side_in[0])
    north_far.wait_recv()
    bx[north_rows, 0:cols] = row_in[1]
    pl.when(jnp.logical_not(bottom))(north_near.wait_recv)
    bx[0:PAD, 0:cols] = row_in[0]
    corners.wait_recv()
    lane = lane_index((8, TILE))
    bx[north_rows, ghost] = jnp.where(lane < TILE // 2, corner_in[1, 1], corner_in[1, 0])
    bx[0:PAD, ghost] = jnp.where(lane < TILE // 2, corner_in[0, 1], corner_in[0, 0])

    height, width = bx.shape

    def operator(field):
        sides = pltpu.roll(field, 1, 1) + pltpu.roll(field, width - 1, 1)
        triple = field + 0.5 * sides
        ends = pltpu.roll(triple, 1, 0) + pltpu.roll(triple, height - 1, 0)
        return cw[...] * field - sides - ends

    zero = lv[...] * bx[...]
    image_zero = operator(zero)
    one = lv[...] * image_zero - zero
    image_one = operator(one)
    two = 2.0 * (lv[...] * image_one - one) - zero
    image_two = operator(two)

    def inner(value):
        return value[own, 0:cols]

    base = [inner(zero), inner(one), inner(two)]
    images = [inner(image_zero), inner(image_one), inner(image_two)]
    source = src_ref[...]
    pairs = [
        (base[0], images[0]), (base[1], images[0]), (base[2], images[0]),
        (base[1], images[1]), (base[2], images[1]), (base[2], images[2]),
        (base[0], source), (base[1], source), (base[2], source),
    ]
    part[8:16, :] = jnp.zeros((8, TILE), F32)
    for i, (x, y) in enumerate(pairs):
        line = jnp.sum(x * y, axis=0, keepdims=True)
        part[i : i + 1, :] = sum(line[:, t : t + TILE] for t in range(0, cols, TILE))
    over_lon = [
        copy_to(part, lon_in.at[d], lon_send.at[d], lon_recv.at[d], peer, lat)
        for d, peer in enumerate(lon_peers)
    ]
    for copy in over_lon:
        copy.start()
    for copy in over_lon:
        copy.wait_recv()
    joint[...] = part[...] + jnp.sum(lon_in[...], axis=0)
    over_lat = [
        copy_to(joint, lat_in.at[d], lat_send.at[d], lat_recv.at[d], lon, peer)
        for d, peer in enumerate(lat_peers)
    ]
    for copy in over_lat:
        copy.start()
    for copy in over_lat:
        copy.wait_recv()
    totals = jnp.sum(joint[...] + jnp.sum(lat_in[...], axis=0), axis=1, keepdims=True)
    g00, g01, g02, g11, g12, g22, d0, d1, d2 = (totals[i : i + 1, :] for i in range(9))
    small = 1e-9 * g00
    l10, l20 = g01 / g00, g02 / g00
    pivot_one = g11 - l10 * g01
    inverse_one = jnp.where(pivot_one > small, 1.0 / pivot_one, 0.0)
    cross = g12 - l20 * g01
    l21 = cross * inverse_one
    pivot_two = g22 - l20 * g02 - l21 * cross
    inverse_two = jnp.where(pivot_two > small, 1.0 / pivot_two, 0.0)
    y1 = d1 - l10 * d0
    y2 = d2 - l20 * d0 - l21 * y1
    c2 = y2 * inverse_two
    c1 = y1 * inverse_one - l21 * c2
    c0 = d0 / g00 - l10 * c1 - l20 * c2
    out_ref[...] = c0 * base[0] + c1 * base[1] + c2 * base[2]

    to_west.wait_send()
    to_east.wait_send()
    north_far.wait_send()
    pl.when(jnp.logical_not(bottom))(south.wait_send)
    corners.wait_send()
    for copy in over_lon + over_lat:
        copy.wait_send()


def shards(
    lons, lats,
    tracers, east_velocity, north_velocity, vertical_diffusivity,
    depth_levels, ocean_blocks, forcing, surface_coupling,
):
    levels, rows, cols = tracers.shape[1:]
    lay = Layout(levels)
    high, wide, tiles = rows + 2 * PAD, cols + TILE, cols // TILE
    dma = pltpu.SemaphoreType.DMA
    strip = jax.ShapeDtypeStruct((lay.rows, cols), F32)
    bf16 = jnp.bfloat16
    plane = jax.ShapeDtypeStruct((rows, cols), F32)
    ghosts, south, north, depth, weight = pl.pallas_call(
        functools.partial(ghost_kernel, lons, lats, levels),
        out_shape=(jax.ShapeDtypeStruct((2, high, TILE), F32), strip, strip, plane, plane),
        in_specs=[HBM, HBM, HBM, HBM, pl.BlockSpec(memory_space=pltpu.SMEM), HBM],
        out_specs=(VMEM,) * 5,
        scratch_shapes=[
            pltpu.VMEM((rows, cols), jnp.int32),
            pltpu.VMEM((rows, cols), F32),
            pltpu.VMEM((2, levels, rows, TILE), F32),
            pltpu.VMEM((2, levels, rows, TILE), F32),
            pltpu.VMEM((2, levels, 8, cols), F32),
            pltpu.VMEM((2, levels, 8, cols), F32),
            pltpu.VMEM((levels, rows, TILE), bf16),
            pltpu.VMEM((levels, rows, TILE), bf16),
            pltpu.VMEM((levels, 16, cols), bf16),
            pltpu.VMEM((levels, 16, cols), bf16),
            pltpu.VMEM((rows, TILE), F32),
            pltpu.VMEM((rows, TILE), F32),
            pltpu.VMEM((lay.rows, cols), F32),
            pltpu.VMEM((lay.rows, cols), F32),
            pltpu.VMEM((2, PAD, TILE), F32),
            pltpu.VMEM((2, 2, PAD, TILE), F32),
            pltpu.VMEM((2, rows, TILE), F32),
            pltpu.VMEM((lay.rows, cols), F32),
            pltpu.VMEM((lay.rows, cols), F32),
            dma((10,)), dma((4,)), dma((4,)), dma((4,)), dma((4,)),
        ],
        compiler_params=pltpu.CompilerParams(
            collective_id=0, has_side_effects=True, vmem_limit_bytes=61 << 20
        ),
        name="ghosts",
    )(tracers, east_velocity, north_velocity, depth_levels, ocean_blocks, surface_coupling)
    new_tracers, source = pl.pallas_call(
        functools.partial(column_kernel, levels),
        out_shape=(
            jax.ShapeDtypeStruct(tracers.shape, F32),
            jax.ShapeDtypeStruct((rows, cols), F32),
        ),
        in_specs=[HBM] * 5 + [VMEM] * 4,
        out_specs=(HBM, VMEM),
        scratch_shapes=[
            pltpu.VMEM((rows, cols), F32),
            pltpu.VMEM((2, levels, high, wide), F32),
            pltpu.VMEM((levels, rows, cols), bf16),
            pltpu.VMEM((levels, rows, cols), bf16),
            pltpu.VMEM((levels, rows, cols), bf16),
            pltpu.VMEM((levels, tiles, high, TILE), F32),
            pltpu.VMEM((tiles + 1, rows, TILE), F32),
            pltpu.VMEM((tiles + 1, high, TILE), F32),
            pltpu.VMEM((tiles + 1, high, TILE), F32),
            pltpu.VMEM((2, tiles + 1, high, TILE), F32),
            pltpu.VMEM((2, tiles + 1, high, TILE), F32),
            pltpu.VMEM((tiles + 1, high, TILE), F32),
            pltpu.VMEM((levels + 1, rows, cols), F32),
            pltpu.VMEM((2, levels + 1, rows, cols), F32),
            pltpu.VMEM((rows, cols), F32),
            dma((4, levels)), dma((levels,)), dma,
        ],
        compiler_params=pltpu.CompilerParams(vmem_limit_bytes=61 << 20),
        name="columns",
    )(tracers, east_velocity, north_velocity, vertical_diffusivity, forcing, depth, ghosts, south, north)
    surface = pl.pallas_call(
        functools.partial(solve_kernel, lons, lats, levels),
        out_shape=jax.ShapeDtypeStruct((rows, cols), F32),
        in_specs=[VMEM] * 6,
        out_specs=VMEM,
        scratch_shapes=[
            pltpu.VMEM((high, wide), F32),
            pltpu.VMEM((high, wide), F32),
            pltpu.VMEM((high, wide), F32),
            pltpu.VMEM((2, rows, TILE), F32),
            pltpu.VMEM((8, cols), F32),
            pltpu.VMEM((2, 8, cols), F32),
            pltpu.VMEM((2, 2, 8, TILE), F32),
            pltpu.VMEM((16, TILE), F32),
            pltpu.VMEM((lons - 1, 16, TILE), F32),
            pltpu.VMEM((16, TILE), F32),
            pltpu.VMEM((lats - 1, 16, TILE), F32),
            dma((4,)), dma((4,)), dma((4,)), dma((4,)),
            dma((lons - 1,)), dma((lons - 1,)), dma((lats - 1,)), dma((lats - 1,)),
        ],
        compiler_params=pltpu.CompilerParams(
            collective_id=1, has_side_effects=True, vmem_limit_bytes=32 << 20
        ),
        name="surface",
    )(source, depth, weight, ghosts, south, north)
    return new_tracers, surface


def solution(mesh):
    flat = P("lat", "lon")
    deep = P(None, "lat", "lon")
    tracer = P(None, None, "lat", "lon")
    return jax.shard_map(
        functools.partial(shards, mesh.shape["lon"], mesh.shape["lat"]),
        mesh=mesh,
        in_specs=(tracer, deep, deep, deep, flat, flat, flat, flat),
        out_specs=(tracer, flat),
        check_vma=False,
    )
```

```python
import functools

import jax
import jax.numpy as jnp
from jax import lax
from jax.experimental import pallas as pl
from jax.experimental.pallas import tpu as pltpu
from jax.sharding import PartitionSpec as P

F32 = jnp.float32
MESH = pl.DeviceIdType.MESH
VMEM = pl.BlockSpec(memory_space=pltpu.VMEM)
HBM = pl.BlockSpec(memory_space=pltpu.HBM)
PAD = 8
TILE = 128


def lane_index(shape):
    return lax.broadcasted_iota(jnp.int32, shape, len(shape) - 1)


def flip_tile(value):
    lane = lane_index(value.shape)
    for bit in range(7):
        step = 1 << bit
        value = jnp.where(
            lane & step != 0, pltpu.roll(value, step, 1), pltpu.roll(value, TILE - step, 1)
        )
    return value


def flip_row(value):
    tiles = value.shape[1] // TILE
    return jnp.concatenate(
        [flip_tile(value[:, t * TILE : (t + 1) * TILE]) for t in reversed(range(tiles))], axis=1
    )


def shift_lanes(value, by):
    width = value.shape[1]
    by = by % width
    return value if by == 0 else pltpu.roll(value, by, 1)


class Layout:
    def __init__(self, levels):
        self.levels = levels
        self.speed = 4 * levels
        self.depth = 5 * levels
        self.weight = 5 * levels + 3
        self.count = 5 * levels + 6
        self.rows = -(-self.count // 8) * 8


def copy_to(src, dst, send, recv, lon, lat):
    return pltpu.make_async_remote_copy(
        src_ref=src,
        dst_ref=dst,
        send_sem=send,
        recv_sem=recv,
        device_id={"lon": lon, "lat": lat},
        device_id_type=MESH,
    )


def greet(barrier, lon, lat):
    pl.semaphore_signal(barrier, inc=1, device_id={"lon": lon, "lat": lat}, device_id_type=MESH)


class Corners:
    def __init__(self, lons, lats, sources, turned, dst, send, recv):
        lon, lat = lax.axis_index("lon"), lax.axis_index("lat")
        east, west = lax.rem(lon + 1, lons), lax.rem(lon + lons - 1, lons)
        self.top, self.bottom = lat == lats - 1, lat == 0
        far_first, far_last = lax.rem(lons - lon, lons), lax.rem(2 * lons - 2 - lon, lons)
        self.own_first = jnp.logical_and(self.top, far_first == lon)
        self.own_last = jnp.logical_and(self.top, far_last == lon)
        self.turned, self.dst = turned, dst
        high_first, high_last, low_first, low_last = sources
        turned_first, turned_last = turned
        self.up_last = copy_to(high_last, dst.at[0, 0], send.at[0], recv.at[0], east, lat + 1)
        self.up_first = copy_to(high_first, dst.at[0, 1], send.at[1], recv.at[1], west, lat + 1)
        self.far_first = copy_to(turned_first, dst.at[1, 0], send.at[1], recv.at[2], far_first, lat)
        self.far_last = copy_to(turned_last, dst.at[1, 1], send.at[0], recv.at[3], far_last, lat)
        self.down_last = copy_to(low_last, dst.at[1, 0], send.at[2], recv.at[2], east, lat - 1)
        self.down_first = copy_to(low_first, dst.at[1, 1], send.at[3], recv.at[3], west, lat - 1)

    def start(self):
        @pl.when(jnp.logical_not(self.top))
        def _():
            self.up_last.start()
            self.up_first.start()

        @pl.when(jnp.logical_not(self.bottom))
        def _():
            self.down_last.start()
            self.down_first.start()

        pl.when(jnp.logical_and(self.top, jnp.logical_not(self.own_first)))(self.far_first.start)
        pl.when(jnp.logical_and(self.top, jnp.logical_not(self.own_last)))(self.far_last.start)

        @pl.when(self.own_first)
        def _():
            self.dst[1, 0] = self.turned[0][...]

        @pl.when(self.own_last)
        def _():
            self.dst[1, 1] = self.turned[1][...]

        @pl.when(self.bottom)
        def _():
            self.dst[0] = jnp.zeros_like(self.dst[0])

    def wait_recv(self):
        @pl.when(jnp.logical_not(self.bottom))
        def _():
            self.up_last.wait_recv()
            self.up_first.wait_recv()

        pl.when(jnp.logical_not(self.own_first))(self.far_first.wait_recv)
        pl.when(jnp.logical_not(self.own_last))(self.far_last.wait_recv)

    def wait_send(self):
        pl.when(jnp.logical_not(self.own_last))(self.up_last.wait_send)
        pl.when(jnp.logical_not(self.own_first))(self.up_first.wait_send)

        @pl.when(jnp.logical_not(self.bottom))
        def _():
            self.down_last.wait_send()
            self.down_first.wait_send()


def ghost_kernel(
    lons, lats, levels,
    tr_ref, u_ref, v_ref, depth_hbm, ocean_ref, coupling_hbm,
    g_out, rs_out, rn_out, lev_ref, cw_ref,
    depth_ref, coupling_ref, t_w, t_e, t_s, t_n, u_w, u_e, v_s, v_n,
    p_w, p_e, r_s, r_n, turned, corner_in, g_in, rs_in, rn_in,
    local_sem, send_sem, recv_sem, corner_send, corner_recv,
):
    lay = Layout(levels)
    lon, lat = lax.axis_index("lon"), lax.axis_index("lat")
    rows, cols = depth_ref.shape
    east, west = lax.rem(lon + 1, lons), lax.rem(lon + lons - 1, lons)
    mirror = lons - 1 - lon
    top = lat == lats - 1
    bottom = lat == 0
    locals_ = [
        pltpu.make_async_copy(src, dst, local_sem.at[i])
        for i, (src, dst) in enumerate(
            (
                (depth_hbm, depth_ref),
                (coupling_hbm, coupling_ref),
                (tr_ref.at[:, :, 0:8, :], t_s),
                (tr_ref.at[:, :, rows - 8 : rows, :], t_n),
                (v_ref.at[:, 0:16, :], v_s),
                (v_ref.at[:, rows - 16 : rows, :], v_n),
                (tr_ref.at[:, :, :, 0:TILE], t_w),
                (tr_ref.at[:, :, :, cols - TILE : cols], t_e),
                (u_ref.at[:, :, 0:TILE], u_w),
                (u_ref.at[:, :, cols - TILE : cols], u_e),
            )
        )
    ]
    for copy in locals_:
        copy.start()
    barrier = pltpu.get_barrier_semaphore()
    greet(barrier, east, lat)
    greet(barrier, west, lat)

    @pl.when(top)
    def _():
        greet(barrier, mirror, lat)

        greet(barrier, lax.rem(lons - lon, lons), lat)
        greet(barrier, lax.rem(2 * lons - 2 - lon, lons), lat)

    @pl.when(jnp.logical_not(top))
    def _():
        for peer in (lon, east, west):
            greet(barrier, peer, lat + 1)

    @pl.when(jnp.logical_not(bottom))
    def _():
        for peer in (lon, east, west):
            greet(barrier, peer, lat - 1)

    @pl.when(bottom)
    def _():
        rs_in[...] = jnp.zeros_like(rs_in)

    for copy in locals_[0:2]:
        copy.wait()
    row = lax.broadcasted_iota(jnp.int32, (rows, cols), 0)
    col = lane_index((rows, cols))
    tall, broad = rows // ocean_ref.shape[0], cols // ocean_ref.shape[1]
    cells = jnp.zeros((rows, cols), jnp.int32)
    for i in range(ocean_ref.shape[0]):
        for j in range(ocean_ref.shape[1]):
            inside = (row >= i * tall) & (row < (i + 1) * tall) & (col >= j * broad) & (col < (j + 1) * broad)
            cells = jnp.where(inside, ocean_ref[i, j], cells)
    lev_ref[...] = jnp.where(cells > 0, depth_ref[...], 0).astype(F32)
    cw_ref[...] = 6.0 + coupling_ref[...]
    for copy in locals_[2:6]:
        copy.wait()
    tail = 8 * (lay.depth // 8)
    r_s[tail:, :] = jnp.zeros_like(r_s[tail:, :])
    r_n[tail:, :] = jnp.zeros_like(r_n[tail:, :])
    for a in range(2):
        for k in range(levels):
            s = 2 * (a * levels + k)
            r_s[s : s + 2, :] = t_s[a, k, 0:2, :]
    for k in range(levels):
        r_s[lay.speed + k : lay.speed + k + 1, :] = v_s[k].astype(F32)[0:1, :]
    r_s[lay.depth : lay.depth + 3, :] = lev_ref[0:3, :]
    r_s[lay.weight : lay.weight + 3, :] = cw_ref[0:3, :]

    @pl.when(jnp.logical_not(top))
    def _():
        for a in range(2):
            for k in range(levels):
                s = 2 * (a * levels + k)
                r_n[s : s + 2, :] = t_n[a, k, 6:8, :]
        for k in range(levels):
            r_n[lay.speed + k : lay.speed + k + 1, :] = v_n[k].astype(F32)[15:16, :]
        r_n[lay.depth : lay.depth + 3, :] = lev_ref[rows - 3 : rows, :]
        r_n[lay.weight : lay.weight + 3, :] = cw_ref[rows - 3 : rows, :]

    @pl.when(top)
    def _():
        for a in range(2):
            for k in range(levels):
                s = 2 * (a * levels + k)
                r_n[s : s + 1, :] = t_n[a, k, 7:8, :]
                r_n[s + 1 : s + 2, :] = t_n[a, k, 6:7, :]
        for k in range(levels):
            r_n[lay.speed + k : lay.speed + k + 1, :] = -v_n[k].astype(F32)[15:16, :]
        for j in range(3):
            r_n[lay.depth + j : lay.depth + j + 1, :] = lev_ref[rows - 1 - j : rows - j, :]
            r_n[lay.weight + j : lay.weight + j + 1, :] = cw_ref[rows - 1 - j : rows - j, :]
        r_n[...] = flip_row(r_n[...])

    @pl.when(bottom)
    def _():
        pl.semaphore_wait(barrier, 5)

    @pl.when(top)
    def _():
        pl.semaphore_wait(barrier, 8)

    @pl.when(jnp.logical_not(jnp.logical_or(top, bottom)))
    def _():
        pl.semaphore_wait(barrier, 8)

    north_far = copy_to(r_n, rn_in, send_sem.at[0], recv_sem.at[0], mirror, lat)
    north_near = copy_to(r_n, rs_in, send_sem.at[0], recv_sem.at[1], lon, lat + 1)
    south = copy_to(r_s, rn_in, send_sem.at[1], recv_sem.at[0], lon, lat - 1)
    pl.when(top)(north_far.start)
    pl.when(jnp.logical_not(top))(north_near.start)
    pl.when(jnp.logical_not(bottom))(south.start)

    for copy in locals_[6:]:
        copy.wait()
    lane = lane_index((rows, TILE))
    back = TILE - 1 - lane
    first, last = jnp.zeros((rows, TILE), F32), jnp.zeros((rows, TILE), F32)
    for a in range(2):
        for k in range(levels):
            s = 2 * (a * levels + k)
            first = jnp.where(lane >> 1 == s // 2, shift_lanes(t_w[a, k], s), first)
            last = jnp.where(back >> 1 == s // 2, shift_lanes(t_e[a, k], -s), last)
    for k in range(levels):
        s = lay.speed + k
        first = jnp.where(lane == s, shift_lanes(u_w[k].astype(F32), s), first)
        last = jnp.where(back == s, shift_lanes(u_e[k].astype(F32), -s), last)
    for ref, s in ((lev_ref, lay.depth), (cw_ref, lay.weight)):
        inside = jnp.logical_and(lane >= s, lane < s + 3)
        first = jnp.where(inside, shift_lanes(ref[:, 0:TILE], s), first)
        inside = jnp.logical_and(back >= s, back < s + 3)
        last = jnp.where(inside, shift_lanes(ref[:, cols - TILE : cols], -s), last)
    p_w[...] = first
    p_e[...] = last
    own = slice(PAD, PAD + rows)
    to_west = copy_to(p_w, g_in.at[1], send_sem.at[2], recv_sem.at[2], west, lat)
    to_east = copy_to(p_e, g_in.at[0], send_sem.at[3], recv_sem.at[3], east, lat)
    to_west.start()
    to_east.start()

    @pl.when(top)
    def _():
        for side, value in enumerate((first, last)):
            back_tile = flip_tile(value[rows - PAD : rows, :])
            for j in range(PAD):
                turned[side, j : j + 1, :] = back_tile[PAD - 1 - j : PAD - j, :]

    corners = Corners(
        lons, lats,
        (p_w.at[rows - PAD : rows, :], p_e.at[rows - PAD : rows, :], p_w.at[0:PAD, :], p_e.at[0:PAD, :]),
        (turned.at[0], turned.at[1]),
        corner_in, corner_send, corner_recv,
    )
    corners.start()
    north_far.wait_recv()
    rn_out[...] = rn_in[...]
    pl.when(jnp.logical_not(bottom))(north_near.wait_recv)
    rs_out[...] = rs_in[...]
    to_west.wait_recv()
    to_east.wait_recv()
    g_out[:, own, :] = g_in[...]
    corners.wait_recv()
    g_out[:, 0:PAD, :] = corner_in[0]
    g_out[:, PAD + rows : 2 * PAD + rows, :] = corner_in[1]
    north_far.wait_send()
    to_west.wait_send()
    to_east.wait_send()
    pl.when(jnp.logical_not(bottom))(south.wait_send)
    corners.wait_send()


def unpacked(g_ref, slot):
    lane = lane_index(g_ref.shape[1:])
    return jnp.where(
        lane < TILE // 2,
        pltpu.roll(g_ref[1], TILE - slot, 1),
        pltpu.roll(g_ref[0], slot, 1),
    )


def column_kernel(
    levels,
    tr_ref, u_ref, v_ref, kd_ref, forcing_hbm, lev_ref, g_ref, rs_ref, rn_ref,
    out_ref, src_ref,
    forcing_ref, tr, u, v, kd, vx, ux, lv, mk, q, lap, sm, ratio, red, coup,
    in_sem, out_sem, forcing_sem,
):
    lay = Layout(levels)
    rows, cols = lev_ref.shape
    tiles = cols // TILE
    own = slice(PAD, PAD + rows)
    ghost = slice(cols, cols + TILE)

    def inputs(k):
        return (
            pltpu.make_async_copy(tr_ref.at[:, k], tr.at[:, k, own, 0:cols], in_sem.at[0, k]),
            pltpu.make_async_copy(u_ref.at[k], u.at[k], in_sem.at[1, k]),
            pltpu.make_async_copy(v_ref.at[k], v.at[k], in_sem.at[2, k]),
            pltpu.make_async_copy(kd_ref.at[k], kd.at[k], in_sem.at[3, k]),
        )

    def outputs(k):
        return pltpu.make_async_copy(red.at[:, k + 1], out_ref.at[:, k], out_sem.at[k])

    for k in range(levels):
        for copy in inputs(k):
            copy.start()
    forcing_copy = pltpu.make_async_copy(forcing_hbm, forcing_ref, forcing_sem)
    forcing_copy.start()
    for k in range(levels):
        for a in range(2):
            s = 2 * (a * levels + k)
            tr[a, k, PAD - 2 : PAD, 0:cols] = rs_ref[s : s + 2, :]
            tr[a, k, PAD + rows : PAD + rows + 2, 0:cols] = rn_ref[s : s + 2, :]
        s = lay.speed + k
        for t in range(tiles):
            part = slice(t * TILE, (t + 1) * TILE)
            vx[k, t, PAD - 1 : PAD, :] = rs_ref[s : s + 1, part]
            vx[k, t, PAD + rows : PAD + rows + 1, :] = rn_ref[s : s + 1, part]
    for t in range(tiles):
        part = slice(t * TILE, (t + 1) * TILE)
        lv[t, 0:PAD] = jnp.zeros((PAD, TILE), F32)
        lv[t, PAD + rows :] = jnp.zeros((PAD, TILE), F32)
        lv[t, own] = lev_ref[:, part]
        lv[t, PAD - 3 : PAD] = rs_ref[lay.depth : lay.depth + 3, part]
        lv[t, PAD + rows : PAD + rows + 3] = rn_ref[lay.depth : lay.depth + 3, part]
    lv[tiles] = unpacked(g_ref, lay.depth)
    coup[...] = jnp.zeros_like(coup)
    ratio[0] = jnp.zeros_like(ratio[0])
    red[:, 0] = jnp.zeros_like(red[:, 0])
    lane = lane_index((8, TILE))
    lane_last, lane_first = lane == TILE - 1, lane == 0

    def right(parts):
        turned = [pltpu.roll(x, TILE - 1, 1) for x in parts]
        return [jnp.where(lane_last, turned[(t + 1) % (tiles + 1)], turned[t]) for t in range(tiles + 1)]

    def left(parts):
        turned = [pltpu.roll(x, 1, 1) for x in parts]
        return [jnp.where(lane_first, turned[(t + tiles) % (tiles + 1)], turned[t]) for t in range(tiles + 1)]

    for copy in inputs(0):
        copy.wait()

    def down(k, carry):
        later = jnp.minimum(k + 1, levels - 1)

        @pl.when(k + 1 < levels)
        def _():
            for copy in inputs(later):
                copy.wait()

        level = k.astype(F32)
        for t in range(tiles):
            ux[t] = u[k, :, t * TILE : (t + 1) * TILE].astype(F32)
            vx[k, t, own] = v[k, :, t * TILE : (t + 1) * TILE].astype(F32)
        ux[tiles] = unpacked(g_ref, lay.speed + k)[own]
        for a in range(2):
            tr[a, k, :, ghost] = unpacked(g_ref, 2 * (a * levels + k))
        for c in range(0, rows + 2 * PAD, 8):
            here = slice(c, c + 8)
            for t in range(tiles + 1):
                wet = jnp.where(lv[t, here] > level, 1.0, 0.0)
                mk[t, here] = wet
                for a in range(2):
                    q[a, t, here] = wet * tr[a, k, here, t * TILE : (t + 1) * TILE]
        every = range(tiles + 1)
        for c in range(0, rows + 8, 8):
            base = c + PAD - 1
            mid, low, high = slice(base, base + 8), slice(base - 1, base + 7), slice(base + 1, base + 9)
            wet = [mk[t, mid] for t in every]
            e, w = right(wet), left(wet)
            total = [e[t] + w[t] + mk[t, low] + mk[t, high] for t in every]
            rate = [0.01 * x for x in wet]
            for t in every:
                sm[t, c : c + 8] = total[t]
            for a in range(2):
                centre = [q[a, t, mid] for t in every]
                e, w = right(centre), left(centre)
                for t in every:
                    around = e[t] + w[t] + q[a, t, low] + q[a, t, high]
                    lap[a, t, c : c + 8] = rate[t] * (around - centre[t] * total[t])
        for c in range(0, rows, 8):
            base = c + PAD
            mid, low, high = slice(base, base + 8), slice(base - 1, base + 7), slice(base + 1, base + 9)
            here = slice(c, c + 8)
            if c % 16 == 0:
                mixing = kd[later, c : c + 16].astype(F32)
            wet = [mk[t, mid] for t in every]
            speed = [ux[t, here] for t in every]
            wet_e, speed_e = right(wet), right(speed)
            face = [0.0625 * (speed[t] + speed_e[t]) * (wet[t] * wet_e[t]) for t in every]
            face_w = left(face)
            shared = []
            for t in range(tiles):
                part = slice(t * TILE, (t + 1) * TILE)
                v_mid = vx[k, t, mid]
                scaled = 0.0625 * wet[t]
                v_north = (v_mid + vx[k, t, high]) * (scaled * mk[t, high])
                v_south = (v_mid + vx[k, t, low]) * (scaled * mk[t, low])
                keep = 1.0 - (face[t] - face_w[t] + v_north - v_south)
                above = coup[here, part]
                below = jnp.where(lv[t, mid] > level + 1.0, mixing[c % 16 : c % 16 + 8, part], 0.0)
                inverse = 1.0 / (1.0 + above + below + above * ratio[k, here, part])
                ratio[k + 1, here, part] = -below * inverse
                coup[here, part] = below
                shared.append((v_north, v_south, keep, above, inverse))
            for a in range(2):
                wide = [q[a, t, mid] for t in every]
                wide_e, wide_w = right(wide), left(wide)
                partial = []
                for t in range(tiles):
                    v_north, v_south, keep, above, inverse = shared[t]
                    part = slice(t * TILE, (t + 1) * TILE)
                    partial.append(
                        wide[t] * keep
                        - face[t] * wide_e[t]
                        + face_w[t] * wide_w[t]
                        - v_north * q[a, t, high]
                        + v_south * q[a, t, low]
                    )
                bent = [lap[a, t, c + 1 : c + 9] for t in every]
                bent_e, bent_w = right(bent), left(bent)
                for t in range(tiles):
                    v_north, v_south, keep, above, inverse = shared[t]
                    part = slice(t * TILE, (t + 1) * TILE)
                    around = bent_e[t] + bent_w[t] + lap[a, t, c + 2 : c + 10] + lap[a, t, c : c + 8]
                    value = partial[t] - wet[t] * (around - bent[t] * sm[t, c + 1 : c + 9])
                    red[a, k + 1, here, part] = (value + above * red[a, k, here, part]) * inverse
        return carry

    lax.fori_loop(0, levels // 2, lambda i, c: down(2 * i + 1, down(2 * i, c)), 0)
    if levels % 2:
        down(jnp.int32(levels - 1), 0)
    outputs(levels - 1).start()
    coup[...] = red[0, levels] - red[1, levels]

    def up(i, carry):
        k = levels - 2 - i
        for c in range(0, rows, 8):
            here = slice(c, c + 8)
            factor = ratio[k + 1, here]
            one = red[0, k + 1, here] - factor * red[0, k + 2, here]
            two = red[1, k + 1, here] - factor * red[1, k + 2, here]
            red[0, k + 1, here] = one
            red[1, k + 1, here] = two
            coup[here] = coup[here] + (one - two)
        outputs(k).start()
        return carry

    lax.fori_loop(0, levels - 1, up, 0)
    forcing_copy.wait()
    src_ref[...] = jnp.where(
        lev_ref[...] > 0.0, forcing_ref[...] + coup[...] * (1.0 / levels), 0.0
    )
    for k in range(levels):
        outputs(k).wait()


def solve_kernel(
    lons, lats, levels,
    src_hbm, lev_ref, cw_ref, g_ref, rs_ref, rn_ref,
    out_ref,
    src_ref, src_sem, lv, cw, bx, side_in, row_n, row_in, corner_in, part, lon_in, joint, lat_in,
    send_sem, recv_sem, corner_send, corner_recv, lon_send, lon_recv, lat_send, lat_recv,
):
    lay = Layout(levels)
    rows, cols = src_ref.shape
    src_copy = pltpu.make_async_copy(src_hbm, src_ref, src_sem)
    src_copy.start()
    lon, lat = lax.axis_index("lon"), lax.axis_index("lat")
    east, west = lax.rem(lon + 1, lons), lax.rem(lon + lons - 1, lons)
    mirror = lons - 1 - lon
    top = lat == lats - 1
    bottom = lat == 0
    own = slice(PAD, PAD + rows)
    north_rows = slice(PAD + rows, 2 * PAD + rows)
    ghost = slice(cols, cols + TILE)
    lon_peers = [lax.rem(lon + d, lons) for d in range(1, lons)]
    lat_peers = [lax.rem(lat + d, lats) for d in range(1, lats)]
    barrier = pltpu.get_barrier_semaphore()
    for peer in lon_peers:
        greet(barrier, peer, lat)
    for peer in lat_peers:
        greet(barrier, lon, peer)

    @pl.when(jnp.logical_not(top))
    def _():
        greet(barrier, east, lat + 1)
        greet(barrier, west, lat + 1)

    @pl.when(jnp.logical_not(bottom))
    def _():
        greet(barrier, east, lat - 1)
        greet(barrier, west, lat - 1)

    src_copy.wait()

    @pl.when(jnp.logical_not(top))
    def _():
        row_n[...] = src_ref[rows - 8 : rows, :]

    @pl.when(top)
    def _():
        turned = flip_row(src_ref[rows - 8 : rows, :])
        for j in range(8):
            row_n[j : j + 1, :] = turned[7 - j : 8 - j, :]

    @pl.when(bottom)
    def _():
        row_in[0] = jnp.zeros_like(row_in[0])

    peers = lons - 1 + lats - 1

    @pl.when(jnp.logical_or(top, bottom))
    def _():
        pl.semaphore_wait(barrier, peers + 2)

    @pl.when(jnp.logical_not(jnp.logical_or(top, bottom)))
    def _():
        pl.semaphore_wait(barrier, peers + 4)

    to_west = copy_to(src_ref.at[:, 0:TILE], side_in.at[1], send_sem.at[2], recv_sem.at[2], west, lat)
    to_east = copy_to(src_ref.at[:, cols - TILE : cols], side_in.at[0], send_sem.at[3], recv_sem.at[3], east, lat)
    to_west.start()
    to_east.start()
    north_far = copy_to(row_n, row_in.at[1], send_sem.at[0], recv_sem.at[0], mirror, lat)
    north_near = copy_to(row_n, row_in.at[0], send_sem.at[0], recv_sem.at[1], lon, lat + 1)
    south = copy_to(src_ref.at[0:8, :], row_in.at[1], send_sem.at[1], recv_sem.at[0], lon, lat - 1)
    pl.when(top)(north_far.start)
    pl.when(jnp.logical_not(top))(north_near.start)
    pl.when(jnp.logical_not(bottom))(south.start)

    corners = Corners(
        lons, lats,
        (
            src_ref.at[rows - 8 : rows, 0:TILE], src_ref.at[rows - 8 : rows, cols - TILE : cols],
            src_ref.at[0:8, 0:TILE], src_ref.at[0:8, cols - TILE : cols],
        ),
        (row_n.at[:, cols - TILE : cols], row_n.at[:, 0:TILE]),
        corner_in, corner_send, corner_recv,
    )
    corners.start()
    for plane, own_ref, slot, empty in ((lv, lev_ref, lay.depth, 0.0), (cw, cw_ref, lay.weight, 1.0)):
        plane[...] = jnp.full(plane.shape, empty, F32)
        plane[own, 0:cols] = own_ref[...]
        plane[PAD - 3 : PAD, 0:cols] = rs_ref[slot : slot + 3, :]
        plane[PAD + rows : PAD + rows + 3, 0:cols] = rn_ref[slot : slot + 3, :]
        plane[:, ghost] = unpacked(g_ref, slot)
    wet = lv[...] > 0.0
    cw[...] = jnp.where(wet, cw[...], 1.0)
    lv[...] = jnp.where(wet, 1.0 / cw[...], 0.0)
    bx[own, 0:cols] = src_ref[...]

    to_west.wait_recv()
    to_east.wait_recv()
    lane = lane_index((rows, TILE))
    bx[own, ghost] = jnp.where(lane < TILE // 2, side_in[1], side_in[0])
    north_far.wait_recv()
    bx[north_rows, 0:cols] = row_in[1]
    pl.when(jnp.logical_not(bottom))(north_near.wait_recv)
    bx[0:PAD, 0:cols] = row_in[0]
    corners.wait_recv()
    lane = lane_index((8, TILE))
    bx[north_rows, ghost] = jnp.where(lane < TILE // 2, corner_in[1, 1], corner_in[1, 0])
    bx[0:PAD, ghost] = jnp.where(lane < TILE // 2, corner_in[0, 1], corner_in[0, 0])

    height, width = bx.shape

    def operator(field):
        sides = pltpu.roll(field, 1, 1) + pltpu.roll(field, width - 1, 1)
        triple = field + 0.5 * sides
        ends = pltpu.roll(triple, 1, 0) + pltpu.roll(triple, height - 1, 0)
        return cw[...] * field - sides - ends

    zero = lv[...] * bx[...]
    image_zero = operator(zero)
    one = lv[...] * image_zero - zero
    image_one = operator(one)
    two = 2.0 * (lv[...] * image_one - one) - zero
    image_two = operator(two)

    def inner(value):
        return value[own, 0:cols]

    base = [inner(zero), inner(one), inner(two)]
    images = [inner(image_zero), inner(image_one), inner(image_two)]
    source = src_ref[...]
    pairs = [
        (base[0], images[0]), (base[1], images[0]), (base[2], images[0]),
        (base[1], images[1]), (base[2], images[1]), (base[2], images[2]),
        (base[0], source), (base[1], source), (base[2], source),
    ]
    part[8:16, :] = jnp.zeros((8, TILE), F32)
    for i, (x, y) in enumerate(pairs):
        line = jnp.sum(x * y, axis=0, keepdims=True)
        part[i : i + 1, :] = sum(line[:, t : t + TILE] for t in range(0, cols, TILE))
    over_lon = [
        copy_to(part, lon_in.at[d], lon_send.at[d], lon_recv.at[d], peer, lat)
        for d, peer in enumerate(lon_peers)
    ]
    for copy in over_lon:
        copy.start()
    for copy in over_lon:
        copy.wait_recv()
    joint[...] = part[...] + jnp.sum(lon_in[...], axis=0)
    over_lat = [
        copy_to(joint, lat_in.at[d], lat_send.at[d], lat_recv.at[d], lon, peer)
        for d, peer in enumerate(lat_peers)
    ]
    for copy in over_lat:
        copy.start()
    for copy in over_lat:
        copy.wait_recv()
    totals = jnp.sum(joint[...] + jnp.sum(lat_in[...], axis=0), axis=1, keepdims=True)
    g00, g01, g02, g11, g12, g22, d0, d1, d2 = (totals[i : i + 1, :] for i in range(9))
    small = 1e-9 * g00
    l10, l20 = g01 / g00, g02 / g00
    pivot_one = g11 - l10 * g01
    inverse_one = jnp.where(pivot_one > small, 1.0 / pivot_one, 0.0)
    cross = g12 - l20 * g01
    l21 = cross * inverse_one
    pivot_two = g22 - l20 * g02 - l21 * cross
    inverse_two = jnp.where(pivot_two > small, 1.0 / pivot_two, 0.0)
    y1 = d1 - l10 * d0
    y2 = d2 - l20 * d0 - l21 * y1
    c2 = y2 * inverse_two
    c1 = y1 * inverse_one - l21 * c2
    c0 = d0 / g00 - l10 * c1 - l20 * c2
    out_ref[...] = c0 * base[0] + c1 * base[1] + c2 * base[2]

    to_west.wait_send()
    to_east.wait_send()
    north_far.wait_send()
    pl.when(jnp.logical_not(bottom))(south.wait_send)
    corners.wait_send()
    for copy in over_lon + over_lat:
        copy.wait_send()


def shards(
    lons, lats,
    tracers, east_velocity, north_velocity, vertical_diffusivity,
    depth_levels, ocean_blocks, forcing, surface_coupling,
):
    levels, rows, cols = tracers.shape[1:]
    lay = Layout(levels)
    high, wide, tiles = rows + 2 * PAD, cols + TILE, cols // TILE
    dma = pltpu.SemaphoreType.DMA
    strip = jax.ShapeDtypeStruct((lay.rows, cols), F32)
    bf16 = jnp.bfloat16
    plane = jax.ShapeDtypeStruct((rows, cols), F32)
    ghosts, south, north, depth, weight = pl.pallas_call(
        functools.partial(ghost_kernel, lons, lats, levels),
        out_shape=(jax.ShapeDtypeStruct((2, high, TILE), F32), strip, strip, plane, plane),
        in_specs=[HBM, HBM, HBM, HBM, pl.BlockSpec(memory_space=pltpu.SMEM), HBM],
        out_specs=(VMEM,) * 5,
        scratch_shapes=[
            pltpu.VMEM((rows, cols), jnp.int32),
            pltpu.VMEM((rows, cols), F32),
            pltpu.VMEM((2, levels, rows, TILE), F32),
            pltpu.VMEM((2, levels, rows, TILE), F32),
            pltpu.VMEM((2, levels, 8, cols), F32),
            pltpu.VMEM((2, levels, 8, cols), F32),
            pltpu.VMEM((levels, rows, TILE), bf16),
            pltpu.VMEM((levels, rows, TILE), bf16),
            pltpu.VMEM((levels, 16, cols), bf16),
            pltpu.VMEM((levels, 16, cols), bf16),
            pltpu.VMEM((rows, TILE), F32),
            pltpu.VMEM((rows, TILE), F32),
            pltpu.VMEM((lay.rows, cols), F32),
            pltpu.VMEM((lay.rows, cols), F32),
            pltpu.VMEM((2, PAD, TILE), F32),
            pltpu.VMEM((2, 2, PAD, TILE), F32),
            pltpu.VMEM((2, rows, TILE), F32),
            pltpu.VMEM((lay.rows, cols), F32),
            pltpu.VMEM((lay.rows, cols), F32),
            dma((10,)), dma((4,)), dma((4,)), dma((4,)), dma((4,)),
        ],
        compiler_params=pltpu.CompilerParams(
            collective_id=0, has_side_effects=True, vmem_limit_bytes=61 << 20
        ),
        name="ghosts",
    )(tracers, east_velocity, north_velocity, depth_levels, ocean_blocks, surface_coupling)
    new_tracers, source = pl.pallas_call(
        functools.partial(column_kernel, levels),
        out_shape=(
            jax.ShapeDtypeStruct(tracers.shape, F32),
            jax.ShapeDtypeStruct((rows, cols), F32),
        ),
        in_specs=[HBM] * 5 + [VMEM] * 4,
        out_specs=(HBM, VMEM),
        scratch_shapes=[
            pltpu.VMEM((rows, cols), F32),
            pltpu.VMEM((2, levels, high, wide), F32),
            pltpu.VMEM((levels, rows, cols), bf16),
            pltpu.VMEM((levels, rows, cols), bf16),
            pltpu.VMEM((levels, rows, cols), bf16),
            pltpu.VMEM((levels, tiles, high, TILE), F32),
            pltpu.VMEM((tiles + 1, rows, TILE), F32),
            pltpu.VMEM((tiles + 1, high, TILE), F32),
            pltpu.VMEM((tiles + 1, high, TILE), F32),
            pltpu.VMEM((2, tiles + 1, high, TILE), F32),
            pltpu.VMEM((2, tiles + 1, high, TILE), F32),
            pltpu.VMEM((tiles + 1, high, TILE), F32),
            pltpu.VMEM((levels + 1, rows, cols), F32),
            pltpu.VMEM((2, levels + 1, rows, cols), F32),
            pltpu.VMEM((rows, cols), F32),
            dma((4, levels)), dma((levels,)), dma,
        ],
        compiler_params=pltpu.CompilerParams(vmem_limit_bytes=61 << 20),
        name="columns",
    )(tracers, east_velocity, north_velocity, vertical_diffusivity, forcing, depth, ghosts, south, north)
    surface = pl.pallas_call(
        functools.partial(solve_kernel, lons, lats, levels),
        out_shape=jax.ShapeDtypeStruct((rows, cols), F32),
        in_specs=[HBM] + [VMEM] * 5,
        out_specs=VMEM,
        scratch_shapes=[
            pltpu.VMEM((rows, cols), F32),
            dma,
            pltpu.VMEM((high, wide), F32),
            pltpu.VMEM((high, wide), F32),
            pltpu.VMEM((high, wide), F32),
            pltpu.VMEM((2, rows, TILE), F32),
            pltpu.VMEM((8, cols), F32),
            pltpu.VMEM((2, 8, cols), F32),
            pltpu.VMEM((2, 2, 8, TILE), F32),
            pltpu.VMEM((16, TILE), F32),
            pltpu.VMEM((lons - 1, 16, TILE), F32),
            pltpu.VMEM((16, TILE), F32),
            pltpu.VMEM((lats - 1, 16, TILE), F32),
            dma((4,)), dma((4,)), dma((4,)), dma((4,)),
            dma((lons - 1,)), dma((lons - 1,)), dma((lats - 1,)), dma((lats - 1,)),
        ],
        compiler_params=pltpu.CompilerParams(
            collective_id=1, has_side_effects=True, vmem_limit_bytes=32 << 20
        ),
        name="surface",
    )(source, depth, weight, ghosts, south, north)
    return new_tracers, surface


def solution(mesh):
    flat = P("lat", "lon")
    deep = P(None, "lat", "lon")
    tracer = P(None, None, "lat", "lon")
    return jax.shard_map(
        functools.partial(shards, mesh.shape["lon"], mesh.shape["lat"]),
        mesh=mesh,
        in_specs=(tracer, deep, deep, deep, flat, flat, flat, flat),
        out_specs=(tracer, flat),
        check_vma=False,
    )
```
